256 devices in a mesh: comp: 128 (over x, z, y), tile: 2 (over core).
Axes of the slice: x: 4, y: 4, z: 8, core: 2. Of those that a mesh axis runs over, the one named last changes fastest.
Arguments:
- adjoint_final: float32 [1152, 128, 256], P('comp', None, 'tile'), may hold values from -6 to 6
- background: float32 [2, 1152, 128, 256], P(None, None, 'comp', 'tile'), as said below
- friction_velocity: float32 [2, 128, 256], P(None, 'comp', 'tile'), may hold values from 0.3 to 1.5
- wind_direction: float32 [2, 128, 256], P(None, 'comp', 'tile'), may hold values from -3.140625 to 3.140625
- refraction_rate: float32 [32, 128, 256], P(None, 'comp', 'tile'), may hold values from -0.45 to 0.45
- courant: float32 [32], replicated, may hold values from 0.2 to 0.63
- growth_rate: float32 [32], replicated, may hold values from 0.05 to 0.25
- dissipation_rate: float32 [32], replicated, may hold values from 0.05 to 0.3
- sea_mask: int32 [128, 256], replicated, may hold values 0 or 1
- interp_index: int32 [4, 128, 256], P(None, 'comp', 'tile'), may hold values from 0 to 2047, as said below
- interp_weight: float32 [4, 128, 256], P(None, 'comp', 'tile'), may hold values from 0 to 1, as said below
Outputs:
- adjoint_initial: float32 [1152, 128, 256], P('comp', None, 'tile')
- stress_gradient: float32 [2048, 2], P(('comp', 'tile'))
The draws below stay inside these ranges and needn't reach their ends.
Inputs may be any that keep to these rules, and one draw needn't show every extreme that they name: `interp_index`: the four forcing cells around the grid cell; forcing cells carry numbers that are a permutation of the forcing grid's cells, the same for all grid cells. `interp_weight`: the four weights of a cell are positive and sum to one. `background`: positive spectra.
All inputs are finite; a program needn't handle non-finite values.
Results may differ from the reference program's by a relative error of at most 0.0001.
Values sent between devices are 32-bit elements; how exact they have to be, the bound alone decides.
No kernel may reach another device: no remote copies, remote signals or barrier semaphores. Data moves between devices by JAX's collectives and lax.ppermute only.
A program may use at most 64 MiB of HBM per device.

```python
import math
import jax
import jax.numpy as jnp
from jax import lax

NDIR = 36
NFREQ = 32
NSTEP = 2
COARSEN = 4
NCOMP = 1152
NX = 128
NY = 256
FX = 32
FY = 64
NF = 2048


def draw_background(key, part):
    keys = jax.random.split(jax.random.fold_in(key, 11), 7)
    shape = (NSTEP, 1, 1, NX, NY)
    sea_freq = jax.random.uniform(keys[0], shape, jnp.float32, 3.0, NFREQ - 4.0)
    sea_dir = jax.random.uniform(keys[1], shape, jnp.float32, -math.pi, math.pi)
    swell_freq = jax.random.uniform(keys[2], shape, jnp.float32, 0.0, NFREQ - 1.0)
    swell_dir = jax.random.uniform(keys[3], shape, jnp.float32, -math.pi, math.pi)
    level = jnp.exp(jax.random.uniform(keys[4], shape, jnp.float32, 0.0, math.log(4.0)))
    swell_share = jax.random.uniform(keys[5], shape, jnp.float32, 0.4, 1.0)
    full = (NSTEP, NFREQ, NDIR, NX, NY)
    rough = jnp.exp(jax.random.uniform(keys[6], full, jnp.float32, math.log(0.5), math.log(2.0)))
    freq = jnp.arange(NFREQ, dtype=jnp.float32)[None, :, None, None, None]
    theta = jnp.arange(NDIR, dtype=jnp.float32)[None, None, :, None, None] * (2.0 * math.pi / NDIR)
    sea_width = NFREQ / 5.0
    swell_width = NFREQ / 8.0
    wind_sea = jnp.exp(-((freq - sea_freq) / sea_width) ** 2) * jnp.maximum(jnp.cos(theta - sea_dir), 0.0) ** 2
    swell = swell_share * jnp.exp(-((freq - swell_freq) / swell_width) ** 2) * jnp.maximum(jnp.cos(theta - swell_dir), 0.0) ** 4
    profile = wind_sea + swell + 0.05
    return (level * (2.2 / NDIR) * profile * rough).reshape(NSTEP, NFREQ * NDIR, NX, NY)


def draw_interp_index(key, part):
    keys = jax.random.split(jax.random.fold_in(key, 23), 4)
    offsets = jax.random.randint(keys[0], (2,), 0, COARSEN)
    row_jitter = jax.random.randint(keys[1], (NX,), 0, 2)
    col_jitter = jax.random.randint(keys[2], (NY,), 0, 2)
    numbering = jax.random.permutation(keys[3], NF).astype(jnp.int32)
    grid_rows = jnp.arange(NX, dtype=jnp.int32)
    grid_cols = jnp.arange(NY, dtype=jnp.int32)
    base_row = jnp.clip((grid_rows + offsets[0]) // COARSEN - row_jitter, 0, FX - 2)
    base_col = jnp.clip((grid_cols + offsets[1]) // COARSEN - col_jitter, 0, FY - 2)
    corner = jnp.arange(4, dtype=jnp.int32)
    row_index = base_row[None, :, None] + (corner // 2)[:, None, None]
    col_index = base_col[None, None, :] + (corner % 2)[:, None, None]
    grid_cell = (row_index * FY + col_index).astype(jnp.int32)
    return jnp.take(numbering, grid_cell).astype(jnp.int32)


def draw_interp_weight(key, part):
    inner = jax.random.fold_in(key, 37)
    raw = jax.random.uniform(inner, (4, NX, NY), jnp.float32, 0.1, 1.0)
    return raw / jnp.sum(raw, axis=0, keepdims=True)


def touch_ends(drawn, key, smallest, largest):
    spot = [jax.random.randint(jax.random.fold_in(key, axis), (), 0, length) for axis, length in enumerate(drawn.shape)]
    widest = drawn.shape.index(max(drawn.shape))
    neighbour = spot[:widest] + [(spot[widest] + 1) % drawn.shape[widest]] + spot[widest + 1:]
    return drawn.at[tuple(spot)].set(smallest).at[tuple(neighbour)].set(largest)


def level_of(own_key, dims, pieces, least, largest):
    factor_of, own = 1.0, jax.random.fold_in(own_key, 6)
    for dim, shards_of in pieces:
        draws = jnp.exp(jax.random.uniform(jax.random.fold_in(own, dim), (shards_of,), jnp.float32, least / len(pieces), largest / len(pieces)))
        factor_of = factor_of * jnp.repeat(draws, dims[dim] // shards_of).reshape([-1 if axis == dim else 1 for axis in range(len(dims))])
    return factor_of


def normal_values(key, shape, width, bound, pieces=(), held_as=jnp.bfloat16):
    values = width * jax.random.normal(key, shape, jnp.float32)
    if pieces:
        values = values * level_of(key, shape, pieces, -0.22, 0.18)
    return jnp.clip(values, -bound, bound).astype(held_as)


def setup_inputs(seed: int = 0) -> dict:
    streams_of = jax.random.split(jax.random.key(seed), 12)
    return {
        "adjoint_final": normal_values(streams_of[0], (NCOMP, NX, NY), 1.0, 6.0, ((0, 128), (2, 2)), jnp.float32),
        "background": draw_background(jax.random.fold_in(streams_of[11], 71), 0),
        "friction_velocity": jnp.clip(jnp.exp(math.log(1.5) - 1.60943787 * jax.random.uniform(streams_of[2], (NSTEP, NX, NY), jnp.float32) ** level_of(streams_of[2], (NSTEP, NX, NY), ((1, 128), (2, 2)), -0.2, 0.2)), 0.3, 1.5),
        "wind_direction": jnp.clip(jax.random.uniform(streams_of[3], (NSTEP, NX, NY), jnp.float32, -3.140625, 3.140625), -3.140625, 3.140625),
        "refraction_rate": jnp.clip(jax.random.uniform(streams_of[4], (NFREQ, NX, NY), jnp.float32, -0.45, 0.45) * level_of(streams_of[4], (NFREQ, NX, NY), ((1, 128), (2, 2)), -0.4, 0.0), -0.45, 0.45),
        "courant": jnp.clip(jnp.exp(jax.random.uniform(streams_of[5], (NFREQ,), jnp.float32, math.log(0.2), math.log(0.63))), 0.2, 0.63),
        "growth_rate": jnp.clip(jnp.exp(jax.random.uniform(streams_of[6], (NFREQ,), jnp.float32, math.log(0.05), math.log(0.25))), 0.05, 0.25),
        "dissipation_rate": jnp.clip(jnp.exp(jax.random.uniform(streams_of[7], (NFREQ,), jnp.float32, math.log(0.05), math.log(0.3))), 0.05, 0.3),
        "sea_mask": touch_ends((jax.random.randint(streams_of[8], (NX, NY), 0, 5) < 4).astype(jnp.int32), jax.random.fold_in(streams_of[8], 1), 0, 1),
        "interp_index": draw_interp_index(jax.random.fold_in(streams_of[11], 71), 0),
        "interp_weight": draw_interp_weight(jax.random.fold_in(streams_of[11], 71), 0),
    }


def spectral_angles():
    return jnp.arange(NDIR, dtype=jnp.int32).astype(jnp.float32) * (2.0 * math.pi / NDIR)


def stencil_adjoint(padded, padded_mask, east_rate, north_rate):
    centre_mask = padded_mask[1:-1, 1:-1]
    face_next_row = centre_mask * padded_mask[2:, 1:-1]
    face_prev_row = centre_mask * padded_mask[:-2, 1:-1]
    face_next_col = centre_mask * padded_mask[1:-1, 2:]
    face_prev_col = centre_mask * padded_mask[1:-1, :-2]
    east_pos = jnp.maximum(east_rate, 0.0)[:, None, None]
    east_neg = jnp.minimum(east_rate, 0.0)[:, None, None]
    north_pos = jnp.maximum(north_rate, 0.0)[:, None, None]
    north_neg = jnp.minimum(north_rate, 0.0)[:, None, None]
    centre = padded[:, 1:-1, 1:-1]
    diagonal = 1.0 - east_pos * face_next_row + east_neg * face_prev_row - north_pos * face_next_col + north_neg * face_prev_col
    result = centre * diagonal
    result = result - east_neg * face_prev_row * padded[:, :-2, 1:-1]
    result = result + east_pos * face_next_row * padded[:, 2:, 1:-1]
    result = result - north_neg * face_prev_col * padded[:, 1:-1, :-2]
    result = result + north_pos * face_next_col * padded[:, 1:-1, 2:]
    return result


def source_adjoint(adjoint, spectrum, friction, wind, sea_cells, growth_rate, dissipation_rate, refraction_rate):
    theta = spectral_angles()
    spread = jnp.maximum(jnp.cos(theta[:, None, None] - wind[None]), 0.0)
    energy = jnp.sum(spectrum, axis=(0, 1)) / NFREQ
    growth = growth_rate[:, None, None, None]
    dissip = dissipation_rate[:, None, None, None]
    damped = jnp.sum(dissip * spectrum * adjoint, axis=(0, 1))
    stress = sea_cells * jnp.sum(growth * spread[None] * spectrum * adjoint, axis=(0, 1))
    diagonal = 1.0 + growth * friction[None, None] * spread[None] - dissip * (energy * energy)[None, None]
    updated = sea_cells * (adjoint * diagonal - (2.0 / NFREQ) * energy * damped)
    turn_pos = jnp.maximum(refraction_rate, 0.0)[:, None]
    turn_neg = jnp.minimum(refraction_rate, 0.0)[:, None]
    keep = (1.0 - jnp.abs(refraction_rate))[:, None]
    turned = keep * updated - turn_neg * jnp.roll(updated, 1, axis=1) + turn_pos * jnp.roll(updated, -1, axis=1)
    return turned, stress


def reference(adjoint_final, background, friction_velocity, wind_direction, refraction_rate, courant, growth_rate, dissipation_rate, sea_mask, interp_index, interp_weight):
    sea_cells = sea_mask.astype(jnp.float32)
    padded_mask = jnp.pad(sea_cells, 1)
    theta = spectral_angles()
    east_rate = courant[:, None] * jnp.cos(theta)[None, :]
    north_rate = courant[:, None] * jnp.sin(theta)[None, :]
    adjoint = adjoint_final.reshape(NFREQ, NDIR, NX, NY)
    corner_cells = interp_index.reshape(-1)
    gradients = [None] * NSTEP

    def propagate_one(operands):
        block, rate_east, rate_north = operands
        padded = jnp.pad(block * sea_cells[None], ((0, 0), (1, 1), (1, 1)))
        return stencil_adjoint(padded, padded_mask, rate_east, rate_north)

    for step in reversed(range(NSTEP)):
        spectrum = background[step].reshape(NFREQ, NDIR, NX, NY)
        adjoint, stress = source_adjoint(adjoint, spectrum, friction_velocity[step], wind_direction[step], sea_cells, growth_rate, dissipation_rate, refraction_rate)
        weighted = (interp_weight * stress[None]).reshape(-1)
        gradients[step] = jax.ops.segment_sum(weighted, corner_cells, num_segments=NF)
        adjoint = lax.map(propagate_one, (adjoint, east_rate, north_rate))
    return adjoint.reshape(NCOMP, NX, NY), jnp.stack(gradients, axis=1)
```

```python
import math

import jax
import jax.numpy as jnp
import numpy as np
from jax import lax
from jax.experimental import pallas as pl
from jax.experimental.pallas import tpu as pltpu
from jax.sharding import PartitionSpec as P

NDIR = 36
NFREQ = 32
NSTEP = 2
NCOMP = NDIR * NFREQ
NX = 128
LANES = 128
LOCAL = 9
QUART = 4
SENT = LOCAL + 1
CELLS = 16

THETA = np.arange(NDIR) * (2.0 * math.pi / NDIR)
COS = np.cos(THETA)
SIN = np.sin(THETA)
EAST = list(range(28, NDIR)) + list(range(0, 10))
WEST = list(range(10, 28))
assert all(COS[d] > 0 for d in EAST) and all(COS[d] < 0 for d in WEST)
ORDER = EAST + WEST
PLACE = {d: p for p, d in enumerate(ORDER)}
HALF = len(EAST) * NFREQ

GROWTH, DISSIP, KEEP, TURN_NEG, TURN_POS, UP, DOWN, RIGHT, LEFT, GAIN0, GAIN1, LOSS0, LOSS1 = range(13)
GAIN, LOSS = (GAIN0, GAIN1), (LOSS0, LOSS1)

PARAMS = pltpu.CompilerParams(vmem_limit_bytes=24 * 1024 * 1024)


def lane_iota(rows):
    return lax.broadcasted_iota(jnp.int32, (rows, LANES), 1)


def sub_iota(rows):
    return lax.broadcasted_iota(jnp.int32, (rows, LANES), 0)


def by_row_kernel(in_ref, out_ref):
    for j in range(LOCAL):
        out_ref[pl.ds(j, NX, stride=LOCAL), :] = in_ref[j]


def prepare_kernel(
    spectrum_ref, friction_ref, wind_ref, refraction_ref, courant_ref, growth_ref, dissip_ref, mask_ref,
    coef_ref, spread_ref, vec_ref, face_ref, rate_ref,
):
    row = lax.axis_index("comp")
    tile = lax.axis_index("tile")
    left_half = mask_ref[:, :LANES].astype(jnp.float32)
    right_half = mask_ref[:, LANES:].astype(jnp.float32)
    first = tile == 0
    own = jnp.where(first, left_half, right_half)
    lane = lane_iota(NX)
    sub = sub_iota(NX)
    other = jnp.where(first, right_half, left_half)
    nxt = jnp.where(lane == LANES - 1, jnp.where(first, pltpu.roll(other, LANES - 1, 1), 0.0), pltpu.roll(own, LANES - 1, 1))
    prv = jnp.where(lane == 0, jnp.where(first, 0.0, pltpu.roll(other, 1, 1)), pltpu.roll(own, 1, 1))
    face_ref[0] = own * jnp.where(sub == NX - 1, 0.0, pltpu.roll(own, NX - 1, 0))
    face_ref[1] = own * jnp.where(sub == 0, 0.0, pltpu.roll(own, 1, 0))
    face_ref[2] = own * nxt
    face_ref[3] = own * prv
    pick = sub == row
    mask = jnp.sum(jnp.where(pick, own, 0.0), axis=0, keepdims=True)
    faces = [face_ref[k, pl.ds(row, 1), :] for k in range(4)]

    sub_f = sub_iota(NFREQ)
    growth = jnp.zeros((NFREQ, LANES), jnp.float32)
    dissip = jnp.zeros((NFREQ, LANES), jnp.float32)
    courant = jnp.zeros((NFREQ, LANES), jnp.float32)
    for f in range(NFREQ):
        at = sub_f == f
        growth = jnp.where(at, growth_ref[f], growth)
        dissip = jnp.where(at, dissip_ref[f], dissip)
        courant = jnp.where(at, courant_ref[f], courant)
    turn = refraction_ref[...]
    coef_ref[GROWTH] = growth
    coef_ref[DISSIP] = dissip
    coef_ref[KEEP] = 1.0 - jnp.abs(turn)
    coef_ref[TURN_NEG] = jnp.minimum(turn, 0.0)
    coef_ref[TURN_POS] = jnp.maximum(turn, 0.0)
    for k, name in enumerate((UP, DOWN, RIGHT, LEFT)):
        coef_ref[name] = courant * faces[k]
    vec_ref[...] = jnp.zeros_like(vec_ref)
    vec_ref[2:3] = mask
    theta = sub_iota(NDIR).astype(jnp.float32) * (2.0 * math.pi / NDIR)
    for n in range(NSTEP):
        total = jnp.zeros((8, LANES), jnp.float32)
        for k in range(NCOMP // 8):
            total = total + spectrum_ref[n, pl.ds(8 * k, 8), :]
        energy = jnp.sum(total, axis=0, keepdims=True) / NFREQ
        vec_ref[n : n + 1] = (2.0 / NFREQ) * energy * mask
        coef_ref[GAIN[n]] = growth * (friction_ref[n : n + 1] * mask)
        coef_ref[LOSS[n]] = mask - dissip * (energy * energy * mask)
        spread_ref[n] = jnp.maximum(jnp.cos(theta - wind_ref[n : n + 1]), 0.0)

    number = (row % QUART) * LOCAL + sub_iota(16)
    angle = number.astype(jnp.float32) * (2.0 * math.pi / NDIR)
    speed = courant_ref[row // QUART]
    rate_ref[0] = speed * jnp.cos(angle)
    rate_ref[1] = speed * jnp.sin(angle)


def source_sums(adjoint_of, spectrum_ref, coef_ref, spread_ref, vec_ref, step):
    damped = jnp.zeros((8, LANES), jnp.float32)
    stress = jnp.zeros((8, LANES), jnp.float32)
    for b in range(NFREQ // 8):
        plain = jnp.zeros((8, LANES), jnp.float32)
        spread = jnp.zeros((8, LANES), jnp.float32)
        for p, d in enumerate(ORDER):
            product = spectrum_ref[step, pl.ds(8 * b * NDIR + d, 8, stride=NDIR), :] * adjoint_of(b, p, d)
            plain = plain + product
            spread = spread + spread_ref[step, d : d + 1, :] * product
        damped = damped + coef_ref[DISSIP, 8 * b : 8 * b + 8] * plain
        stress = stress + coef_ref[GROWTH, 8 * b : 8 * b + 8] * spread
    damped = jnp.sum(damped, axis=0, keepdims=True)
    stress = jnp.sum(stress, axis=0, keepdims=True)
    return vec_ref[step : step + 1] * damped, vec_ref[2:3] * stress


def source_update(adjoint_of, store, coef_ref, spread_ref, shared, step):
    shared = jnp.broadcast_to(shared, (8, LANES))
    for b in range(NFREQ // 8):
        rows = slice(8 * b, 8 * b + 8)
        gain, loss = coef_ref[GAIN[step], rows], coef_ref[LOSS[step], rows]
        keep, neg, pos = coef_ref[KEEP, rows], coef_ref[TURN_NEG, rows], coef_ref[TURN_POS, rows]

        def updated(d):
            return adjoint_of(b, PLACE[d], d) * (loss + gain * spread_ref[step, d : d + 1, :]) - shared

        before, here, first = updated(ORDER[-1]), updated(ORDER[0]), None
        first = here
        for p, d in enumerate(ORDER):
            after = updated(ORDER[p + 1]) if p + 1 < NDIR else first
            store(b, p, d, keep * here - neg * before + pos * after)
            before, here = here, after


def first_source_kernel(
    adjoint_ref, spectrum_ref, coef_ref, spread_ref, vec_ref, east_ref, west_ref, edge_ref, stress_ref
):
    step = NSTEP - 1

    def adjoint_of(b, p, d):
        return adjoint_ref[pl.ds(8 * b * NDIR + d, 8, stride=NDIR), :]

    shared, stress = source_sums(adjoint_of, spectrum_ref, coef_ref, spread_ref, vec_ref, step)
    stress_ref[...] = jnp.broadcast_to(stress, (8, LANES))
    lane = lane_iota(8)
    edges = [jnp.zeros((8, LANES), jnp.float32) for _ in range(NFREQ // 8)]

    def store(b, p, d, value):
        ref, at = (east_ref, p) if p < NDIR // 2 else (west_ref, p - NDIR // 2)
        ref[pl.ds(at * NFREQ + 8 * b, 8), :] = value
        column = value[:, :1] if SIN[d] >= 0 else value[:, LANES - 1 :]
        edges[b] = jnp.where(lane == p, column, edges[b])

    source_update(adjoint_of, store, coef_ref, spread_ref, shared, step)
    for b in range(NFREQ // 8):
        edge_ref[8 * b : 8 * b + 8] = edges[b]


def second_source_kernel(
    east_ref, west_ref, east_next_ref, west_prev_ref, edge_ref, spectrum_ref, coef_ref, spread_ref, vec_ref, stress_ref,
    index_ref, weight_ref, out_ref, held_ref,
):
    step = 0
    lane = lane_iota(8)

    def propagated(b, p, d):
        rows = slice(8 * b, 8 * b + 8)
        ref, near, face, at = (
            (east_ref, east_next_ref, UP, p) if p < NDIR // 2 else (west_ref, west_prev_ref, DOWN, p - NDIR // 2)
        )
        centre = ref[pl.ds(at * NFREQ + 8 * b, 8), :]
        row = near[pl.ds(at * NFREQ + 8 * b, 8), :]
        arrived = edge_ref[rows, p : p + 1]
        if SIN[d] >= 0:
            side, column = RIGHT, jnp.where(lane == LANES - 1, arrived, pltpu.roll(centre, LANES - 1, 1))
        else:
            side, column = LEFT, jnp.where(lane == 0, arrived, pltpu.roll(centre, 1, 1))
        value = (
            centre
            + abs(float(COS[d])) * (coef_ref[face, rows] * (row - centre))
            + abs(float(SIN[d])) * (coef_ref[side, rows] * (column - centre))
        )
        held_ref[pl.ds(p * NFREQ + 8 * b, 8), :] = value
        return value

    shared, stress = source_sums(propagated, spectrum_ref, coef_ref, spread_ref, vec_ref, step)

    cells = jnp.zeros((NX, LANES), jnp.float32)
    sub = sub_iota(NX)
    for corner in range(4):
        index = index_ref[corner : corner + 1, :]
        owner = jnp.where(sub == index // CELLS, 1.0, 0.0)
        cell = index % CELLS
        weight = weight_ref[corner : corner + 1, :]
        values = jnp.where(sub == cell, weight * stress, 0.0)
        values = values + jnp.where(sub == cell + CELLS, weight * stress_ref[:1], 0.0)
        cells = cells + lax.dot_general(
            owner,
            values,
            (((1,), (1,)), ((), ())),
            precision=lax.Precision.HIGHEST,
            preferred_element_type=jnp.float32,
        )
    out_ref[pl.ds(LOCAL, NX, stride=SENT), :] = cells

    def adjoint_of(b, p, d):
        return held_ref[pl.ds(p * NFREQ + 8 * b, 8), :]

    def store(b, p, d, value):
        at = 8 * b * QUART * SENT + d // LOCAL * SENT + d % LOCAL
        out_ref[pl.ds(at, 8, stride=QUART * SENT), :] = value

    source_update(adjoint_of, store, coef_ref, spread_ref, shared, step)


def edges_kernel(arrived_ref, out_ref):
    lane = lane_iota(NX)
    edges = jnp.zeros((NX, LANES), jnp.float32)
    for j in range(LOCAL):
        value = arrived_ref[pl.ds(j, NX, stride=SENT), :]
        edges = jnp.where(lane == j, value[:, :1], edges)
        edges = jnp.where(lane == 16 + j, value[:, LANES - 1 :], edges)
    out_ref[:NX] = edges
    cells = arrived_ref[pl.ds(LOCAL, NX, stride=SENT), :]
    out_ref[NX:] = jnp.broadcast_to(jnp.sum(cells, axis=0, keepdims=True), (8, LANES))


def last_kernel(arrived_ref, mine_ref, edges_ref, face_ref, rate_ref, adjoint_ref, gradient_ref):
    tile = lax.axis_index("tile")
    lane = lane_iota(NX)
    for j in range(LOCAL):
        centre = arrived_ref[pl.ds(j, NX, stride=SENT), :]
        east, north = rate_ref[0, j : j + 1], rate_ref[1, j : j + 1]
        up = pltpu.roll(centre, NX - 1, 0) - centre
        down = pltpu.roll(centre, 1, 0) - centre
        right = jnp.where(lane == LANES - 1, edges_ref[:NX, j : j + 1], pltpu.roll(centre, LANES - 1, 1)) - centre
        left = jnp.where(lane == 0, edges_ref[:NX, 16 + j : 17 + j], pltpu.roll(centre, 1, 1)) - centre
        value = centre + jnp.maximum(east, 0.0) * (face_ref[0] * up) - jnp.minimum(east, 0.0) * (face_ref[1] * down)
        value = value + jnp.maximum(north, 0.0) * (face_ref[2] * right) - jnp.minimum(north, 0.0) * (face_ref[3] * left)
        adjoint_ref[j] = value
    cells = mine_ref[NX : NX + 1] + edges_ref[NX : NX + 1]
    at = lane_iota(8) - sub_iota(8) - tile * (CELLS // 2)
    for n in range(NSTEP):
        gradient_ref[:, n : n + 1] = jnp.sum(jnp.where(at == n * CELLS, cells, 0.0), axis=1, keepdims=True)


def f32(*shape):
    return jax.ShapeDtypeStruct(shape, jnp.float32)


def spec(*spaces):
    return [pl.BlockSpec(memory_space=pltpu.SMEM if s == "s" else pltpu.VMEM) for s in spaces[0]]


def call(kernel, inputs, out_shape, scratch=()):
    single = not isinstance(out_shape, tuple)
    return pl.pallas_call(
        kernel,
        in_specs=spec(inputs),
        out_specs=spec("v")[0] if single else tuple(spec("v" * len(out_shape))),
        out_shape=out_shape,
        scratch_shapes=list(scratch),
        compiler_params=PARAMS,
    )


def shards(
    adjoint_final,
    background,
    friction_velocity,
    wind_direction,
    refraction_rate,
    courant,
    growth_rate,
    dissipation_rate,
    sea_mask,
    interp_index,
    interp_weight,
):
    comp_count = lax.axis_size("comp")
    spectrum = background.reshape(NSTEP, NCOMP, LANES)
    by_row = call(by_row_kernel, "v", f32(NCOMP, LANES))(adjoint_final)
    points = lax.all_to_all(by_row.reshape(NCOMP, 1, LANES), "comp", split_axis=0, concat_axis=0, tiled=True)
    points = points.reshape(NCOMP, LANES)
    coef, spread, vec, face, rate = call(
        prepare_kernel,
        "vvvvsssv",
        (f32(13, NFREQ, LANES), f32(NSTEP, NDIR, LANES), f32(8, LANES), f32(4, NX, LANES), f32(2, 16, LANES)),
    )(
        spectrum,
        friction_velocity.reshape(NSTEP, LANES),
        wind_direction.reshape(NSTEP, LANES),
        refraction_rate.reshape(NFREQ, LANES),
        courant,
        growth_rate,
        dissipation_rate,
        sea_mask,
    )
    east, west, edge, stress = call(
        first_source_kernel, "vvvvv", (f32(HALF, LANES), f32(HALF, LANES), f32(NFREQ, LANES), f32(8, LANES))
    )(points, spectrum, coef, spread, vec)
    swap = [(0, 1), (1, 0)]
    east_next = lax.ppermute(east, "comp", [(i + 1, i) for i in range(comp_count - 1)])
    west_prev = lax.ppermute(west, "comp", [(i, i + 1) for i in range(comp_count - 1)])
    edge = lax.ppermute(edge, "tile", swap)
    sent = call(
        second_source_kernel,
        "vvvvvvvvvvvv",
        f32(NX * SENT, LANES),
        [pltpu.VMEM((NCOMP, LANES), jnp.float32)],
    )(
        east, west, east_next, west_prev, edge, spectrum, coef, spread, vec, stress,
        interp_index.reshape(4, LANES), interp_weight.reshape(4, LANES),
    )
    arrived = lax.all_to_all(sent.reshape(NX * SENT, 1, LANES), "comp", split_axis=0, concat_axis=0, tiled=True)
    arrived = arrived.reshape(NX * SENT, LANES)
    mine = call(edges_kernel, "v", f32(NX + 8, LANES))(arrived)
    theirs = lax.ppermute(mine, "tile", swap)
    return call(last_kernel, "vvvvv", (f32(LOCAL, NX, LANES), f32(8, NSTEP)))(arrived, mine, theirs, face, rate)


def solution(mesh):
    in_specs = (
        P("comp", None, "tile"),
        P(None, None, "comp", "tile"),
        P(None, "comp", "tile"),
        P(None, "comp", "tile"),
        P(None, "comp", "tile"),
        P(),
        P(),
        P(),
        P(),
        P(None, "comp", "tile"),
        P(None, "comp", "tile"),
    )
    out_specs = (P("comp", None, "tile"), P(("comp", "tile"), None))
    return jax.shard_map(shards, mesh=mesh, in_specs=in_specs, out_specs=out_specs, check_vma=False)
```

```python
import math

import jax
import jax.numpy as jnp
import numpy as np
from jax import lax
from jax.experimental import pallas as pl
from jax.experimental.pallas import tpu as pltpu
from jax.sharding import PartitionSpec as P

NDIR = 36
NFREQ = 32
NSTEP = 2
NCOMP = NDIR * NFREQ
NX = 128
LANES = 128
LOCAL = 9
QUART = 4
SENT = LOCAL + 1
CELLS = 16

THETA = np.arange(NDIR) * (2.0 * math.pi / NDIR)
COS = [0.0 if d % 18 == 9 else math.cos(t) for d, t in enumerate(THETA)]
SIN = [0.0 if d % 18 == 0 else math.sin(t) for d, t in enumerate(THETA)]
EAST = list(range(27, NDIR)) + list(range(0, 9))
WEST = list(range(9, 27))
assert all(COS[d] >= 0 for d in EAST) and all(COS[d] <= 0 for d in WEST)
assert all(SIN[d] >= 0 for d in range(18)) and all(SIN[d] <= 0 for d in range(18, 36))
ORDER = EAST + WEST
PLACE = {d: p for p, d in enumerate(ORDER)}
HALF = len(EAST) * NFREQ

GROWTH, DISSIP, KEEP, TURN_NEG, TURN_POS, UP, DOWN, RIGHT, LEFT, GAIN0, GAIN1, LOSS0, LOSS1 = range(13)
GAIN, LOSS = (GAIN0, GAIN1), (LOSS0, LOSS1)
PART = NSTEP * CELLS

PARAMS = pltpu.CompilerParams(vmem_limit_bytes=24 * 1024 * 1024)
WHOLE = pltpu.CompilerParams(vmem_limit_bytes=60 * 1024 * 1024)


def lane_iota(rows):
    return lax.broadcasted_iota(jnp.int32, (rows, LANES), 1)


def sub_iota(rows):
    return lax.broadcasted_iota(jnp.int32, (rows, LANES), 0)


def by_row_kernel(in_ref, out_ref, held_ref, sems):
    copies = [pltpu.make_async_copy(in_ref.at[j], held_ref.at[j], sems.at[j]) for j in range(LOCAL)]
    for copy in copies:
        copy.start()
    for j, copy in enumerate(copies):
        copy.wait()
        out_ref[pl.ds(j, NX, stride=LOCAL), :] = held_ref[j]


def prepare_kernel(
    spectrum_ref, friction_ref, wind_ref, refraction_ref, courant_ref, growth_ref, dissip_ref, mask_ref,
    index_ref, weight_ref, coef_ref, spread_ref, vec_ref, face_ref, owner_ref, cell_ref,
):
    row = lax.axis_index("comp")
    tile = lax.axis_index("tile")
    left_half = mask_ref[:, :LANES].astype(jnp.float32)
    right_half = mask_ref[:, LANES:].astype(jnp.float32)
    first = tile == 0
    own = jnp.where(first, left_half, right_half)
    lane = lane_iota(NX)
    sub = sub_iota(NX)
    other = jnp.where(first, right_half, left_half)
    nxt = jnp.where(lane == LANES - 1, jnp.where(first, pltpu.roll(other, LANES - 1, 1), 0.0), pltpu.roll(own, LANES - 1, 1))
    prv = jnp.where(lane == 0, jnp.where(first, 0.0, pltpu.roll(other, 1, 1)), pltpu.roll(own, 1, 1))
    quarter = row % QUART
    speed = courant_ref[row // QUART]
    up = own * jnp.where(sub == NX - 1, 0.0, pltpu.roll(own, NX - 1, 0))
    down = own * jnp.where(sub == 0, 0.0, pltpu.roll(own, 1, 0))
    right, left = own * nxt, own * prv
    face_ref[0] = speed * jnp.where((quarter == 0) | (quarter == 3), up, down)
    face_ref[1] = speed * jnp.where(quarter < 2, right, left)
    pick = sub == row
    mask, *faces = [
        jnp.sum(jnp.where(pick, value, 0.0), axis=0, keepdims=True) for value in (own, up, down, right, left)
    ]

    sub_f = sub_iota(NFREQ)
    growth = jnp.zeros((NFREQ, LANES), jnp.float32)
    dissip = jnp.zeros((NFREQ, LANES), jnp.float32)
    courant = jnp.zeros((NFREQ, LANES), jnp.float32)
    for f in range(NFREQ):
        at = sub_f == f
        growth = jnp.where(at, growth_ref[f], growth)
        dissip = jnp.where(at, dissip_ref[f], dissip)
        courant = jnp.where(at, courant_ref[f], courant)
    turn = refraction_ref[...]
    coef_ref[GROWTH] = growth
    coef_ref[DISSIP] = dissip
    coef_ref[KEEP] = 1.0 - jnp.abs(turn)
    coef_ref[TURN_NEG] = jnp.minimum(turn, 0.0)
    coef_ref[TURN_POS] = jnp.maximum(turn, 0.0)
    for k, name in enumerate((UP, DOWN, RIGHT, LEFT)):
        coef_ref[name] = courant * faces[k]
    vec_ref[...] = jnp.zeros_like(vec_ref)
    vec_ref[2:3] = mask
    theta = sub_iota(NDIR).astype(jnp.float32) * (2.0 * math.pi / NDIR)
    for n in range(NSTEP):
        total = jnp.zeros((8, LANES), jnp.float32)
        for k in range(NCOMP // 8):
            total = total + spectrum_ref[n, pl.ds(8 * k, 8), :]
        energy = jnp.sum(total, axis=0, keepdims=True) / NFREQ
        vec_ref[n : n + 1] = (2.0 / NFREQ) * energy * mask
        coef_ref[GAIN[n]] = growth * (friction_ref[n : n + 1] * mask)
        coef_ref[LOSS[n]] = mask - dissip * (energy * energy * mask)
        spread_ref[n] = jnp.maximum(jnp.cos(theta - wind_ref[n : n + 1]), 0.0)

    sub_c = sub_iota(PART)
    for corner in range(4):
        lanes = slice(corner * LANES, (corner + 1) * LANES)
        index = index_ref[corner : corner + 1, :]
        owner_ref[:, lanes] = jnp.where(sub == index // CELLS, 1.0, 0.0).astype(jnp.bfloat16)
        cell_ref[:, lanes] = jnp.where(sub_c % CELLS == index % CELLS, weight_ref[corner : corner + 1, :], 0.0)


def source_sums(adjoint_of, spectrum_ref, coef_ref, spread_ref, vec_ref, step):
    damped = jnp.zeros((8, LANES), jnp.float32)
    stress = jnp.zeros((8, LANES), jnp.float32)
    for b in range(NFREQ // 8):
        plain = jnp.zeros((8, LANES), jnp.float32)
        spread = jnp.zeros((8, LANES), jnp.float32)
        for p, d in enumerate(ORDER):
            product = spectrum_ref[step, pl.ds(8 * b * NDIR + d, 8, stride=NDIR), :] * adjoint_of(b, p, d)
            plain = plain + product
            spread = spread + spread_ref[step, d : d + 1, :] * product
        damped = damped + coef_ref[DISSIP, 8 * b : 8 * b + 8] * plain
        stress = stress + coef_ref[GROWTH, 8 * b : 8 * b + 8] * spread
    damped = jnp.sum(damped, axis=0, keepdims=True)
    stress = jnp.sum(stress, axis=0, keepdims=True)
    return vec_ref[step : step + 1] * damped, vec_ref[2:3] * stress


def source_update(adjoint_of, store, coef_ref, spread_ref, shared, step):
    shared = jnp.broadcast_to(shared, (8, LANES))
    for b in range(NFREQ // 8):
        rows = slice(8 * b, 8 * b + 8)
        gain, loss = coef_ref[GAIN[step], rows], coef_ref[LOSS[step], rows]
        keep, neg, pos = coef_ref[KEEP, rows], coef_ref[TURN_NEG, rows], coef_ref[TURN_POS, rows]

        def updated(d):
            return adjoint_of(b, PLACE[d], d) * (loss + gain * spread_ref[step, d : d + 1, :]) - shared

        before, here, first = updated(ORDER[-1]), updated(ORDER[0]), None
        first = here
        for p, d in enumerate(ORDER):
            after = updated(ORDER[p + 1]) if p + 1 < NDIR else first
            store(b, p, d, keep * here - neg * before + pos * after)
            before, here = here, after


def first_source_kernel(
    adjoint_ref, spectrum_ref, coef_ref, spread_ref, vec_ref, moved_ref, one_ref, two_ref, edge_ref, stress_ref
):
    step = NSTEP - 1

    def adjoint_of(b, p, d):
        return adjoint_ref[pl.ds(8 * b * NDIR + d, 8, stride=NDIR), :]

    shared, stress = source_sums(adjoint_of, spectrum_ref, coef_ref, spread_ref, vec_ref, step)
    stress_ref[...] = jnp.broadcast_to(stress, (8, LANES))
    lane = lane_iota(8)
    edges = [jnp.zeros((8, LANES), jnp.float32) for _ in range(NFREQ // 8)]

    def store(b, p, d, value):
        moved_ref[pl.ds(p * NFREQ + 8 * b, 8), :] = value
        column = value[:, :1] if SIN[d] >= 0 else value[:, LANES - 1 :]
        edges[b] = jnp.where(lane == p, column, edges[b])

    source_update(adjoint_of, store, coef_ref, spread_ref, shared, step)
    for b in range(NFREQ // 8):
        edge_ref[8 * b : 8 * b + 8] = edges[b]
    tile = lax.axis_index("tile")

    @pl.when(tile == 0)
    def _():
        one_ref[...] = moved_ref[:HALF]
        two_ref[...] = moved_ref[HALF:]

    @pl.when(tile == 1)
    def _():
        one_ref[...] = moved_ref[HALF:]
        two_ref[...] = moved_ref[:HALF]


def second_source_kernel(
    moved_ref, one_ref, two_ref, edge_ref, spectrum_ref, coef_ref, spread_ref, vec_ref, stress_ref,
    owner_ref, cell_ref, out_ref, held_ref,
):
    step = 0
    lane = lane_iota(8)
    first = jnp.broadcast_to(lax.axis_index("tile"), (8, LANES)) == 0

    def propagated(b, p, d):
        rows = slice(8 * b, 8 * b + 8)
        east = p < NDIR // 2
        face, at = (UP, p) if east else (DOWN, p - NDIR // 2)
        centre = moved_ref[pl.ds(p * NFREQ + 8 * b, 8), :]
        one = one_ref[pl.ds(at * NFREQ + 8 * b, 8), :]
        two = two_ref[pl.ds(at * NFREQ + 8 * b, 8), :]
        row = jnp.where(first, one, two) if east else jnp.where(first, two, one)
        arrived = edge_ref[rows, p : p + 1]
        if SIN[d] >= 0:
            side, column = RIGHT, jnp.where(lane == LANES - 1, arrived, pltpu.roll(centre, LANES - 1, 1))
        else:
            side, column = LEFT, jnp.where(lane == 0, arrived, pltpu.roll(centre, 1, 1))
        value = (
            centre
            + abs(COS[d]) * (coef_ref[face, rows] * (row - centre))
            + abs(SIN[d]) * (coef_ref[side, rows] * (column - centre))
        )
        held_ref[pl.ds(p * NFREQ + 8 * b, 8), :] = value
        return value

    shared, stress = source_sums(propagated, spectrum_ref, coef_ref, spread_ref, vec_ref, step)

    values = jnp.concatenate(
        [
            cell_ref[CELLS * n : CELLS * n + CELLS, :] * jnp.concatenate([row] * 4, axis=1)
            for n, row in enumerate((stress, stress_ref[:1]))
        ],
        axis=0,
    )
    parts = []
    for _ in range(3):
        parts.append(values.astype(jnp.bfloat16))
        values = values - parts[-1].astype(jnp.float32)
    parts.append(jnp.zeros_like(parts[0]))
    cells = lax.dot_general(
        owner_ref[...], jnp.concatenate(parts, axis=0), (((1,), (1,)), ((), ())), preferred_element_type=jnp.float32
    )
    out_ref[pl.ds(LOCAL, NX, stride=SENT), :] = cells

    def adjoint_of(b, p, d):
        return held_ref[pl.ds(p * NFREQ + 8 * b, 8), :]

    def store(b, p, d, value):
        at = 8 * b * QUART * SENT + d // LOCAL * SENT + d % LOCAL
        out_ref[pl.ds(at, 8, stride=QUART * SENT), :] = value

    source_update(adjoint_of, store, coef_ref, spread_ref, shared, step)


def edges_kernel(arrived_ref, out_ref):
    lane = lane_iota(NX)
    quarter = lax.axis_index("comp") % QUART
    for north in (True, False):

        @pl.when((quarter < 2) == north)
        def _():
            edges = jnp.zeros((NX, LANES), jnp.float32)
            for j in range(LOCAL):
                value = arrived_ref[pl.ds(j, NX, stride=SENT), :]
                edges = jnp.where(lane == j, value[:, :1] if north else value[:, LANES - 1 :], edges)
            out_ref[:NX] = edges

    cells = arrived_ref[pl.ds(LOCAL, NX, stride=SENT), :]
    out_ref[NX:] = jnp.broadcast_to(jnp.sum(cells, axis=0, keepdims=True), (8, LANES))


def last_kernel(arrived_ref, mine_ref, edges_ref, face_ref, adjoint_ref, gradient_ref, held_ref, sems):
    tile = lax.axis_index("tile")
    quarter = lax.axis_index("comp") % QUART
    lane = lane_iota(NX)
    copies = [pltpu.make_async_copy(held_ref.at[j], adjoint_ref.at[j], sems.at[j]) for j in range(LOCAL)]
    for q in range(QUART):

        @pl.when(quarter == q)
        def _():
            for j in range(LOCAL):
                d = q * LOCAL + j
                centre = arrived_ref[pl.ds(j, NX, stride=SENT), :]
                arrived = edges_ref[:NX, j : j + 1]
                row = pltpu.roll(centre, NX - 1 if d in EAST else 1, 0)
                if SIN[q * LOCAL + 1] > 0:
                    column = jnp.where(lane == LANES - 1, arrived, pltpu.roll(centre, LANES - 1, 1))
                else:
                    column = jnp.where(lane == 0, arrived, pltpu.roll(centre, 1, 1))
                held_ref[j] = (
                    centre
                    + abs(COS[d]) * (face_ref[0] * (row - centre))
                    + abs(SIN[d]) * (face_ref[1] * (column - centre))
                )
                copies[j].start()

    cells = mine_ref[NX:] + edges_ref[NX:]
    cells = cells + pltpu.roll(cells, LANES - PART, 1) + pltpu.roll(cells, LANES - 2 * PART, 1)
    for n in range(NSTEP):
        at = pltpu.roll(cells, LANES - n * CELLS - tile * (CELLS // 2), 1)
        gradient_ref[n : n + 1, :] = at[:1, : CELLS // 2]
    for copy in copies:
        copy.wait()


def f32(*shape):
    return jax.ShapeDtypeStruct(shape, jnp.float32)


SPACES = {"s": pltpu.SMEM, "v": pltpu.VMEM, "h": pltpu.HBM}


def spec(spaces):
    return [pl.BlockSpec(memory_space=SPACES[space]) for space in spaces]


def call(kernel, inputs, outputs, out_shape, scratch=(), params=PARAMS):
    single = len(outputs) == 1
    return pl.pallas_call(
        kernel,
        in_specs=spec(inputs),
        out_specs=spec(outputs)[0] if single else tuple(spec(outputs)),
        out_shape=out_shape,
        scratch_shapes=list(scratch),
        compiler_params=params,
    )


def shards(
    adjoint_final,
    background,
    friction_velocity,
    wind_direction,
    refraction_rate,
    courant,
    growth_rate,
    dissipation_rate,
    sea_mask,
    interp_index,
    interp_weight,
):
    comp_count = lax.axis_size("comp")
    spectrum = background.reshape(NSTEP, NCOMP, LANES)
    held = [pltpu.VMEM((LOCAL, NX, LANES), jnp.float32), pltpu.SemaphoreType.DMA((LOCAL,))]
    by_row = call(by_row_kernel, "h", "v", f32(NCOMP, LANES), held, WHOLE)(adjoint_final)
    points = lax.all_to_all(by_row.reshape(NCOMP, 1, LANES), "comp", split_axis=0, concat_axis=0, tiled=True)
    points = points.reshape(NCOMP, LANES)
    coef, spread, vec, face, owner, cell = call(
        prepare_kernel,
        "vvvvsssvvv",
        "vvvvvv",
        (
            f32(13, NFREQ, LANES),
            f32(NSTEP, NDIR, LANES),
            f32(8, LANES),
            f32(2, NX, LANES),
            jax.ShapeDtypeStruct((NX, 4 * LANES), jnp.bfloat16),
            f32(PART, 4 * LANES),
        ),
    )(
        spectrum,
        friction_velocity.reshape(NSTEP, LANES),
        wind_direction.reshape(NSTEP, LANES),
        refraction_rate.reshape(NFREQ, LANES),
        courant,
        growth_rate,
        dissipation_rate,
        sea_mask,
        interp_index.reshape(4, LANES),
        interp_weight.reshape(4, LANES),
    )
    moved, one, two, edge, stress = call(
        first_source_kernel,
        "vvvvv",
        "vvvvv",
        (f32(NCOMP, LANES), f32(HALF, LANES), f32(HALF, LANES), f32(NFREQ, LANES), f32(8, LANES)),
    )(points, spectrum, coef, spread, vec)
    swap = [(0, 1), (1, 0)]
    steps = range(comp_count - 1)
    turns = [
        [(2 * (i + 1) + t, 2 * i + t) for i in steps] + [(2 * i + 1 - t, 2 * (i + 1) + 1 - t) for i in steps]
        for t in range(2)
    ]
    one = lax.ppermute(one, ("comp", "tile"), turns[0])
    two = lax.ppermute(two, ("comp", "tile"), turns[1])
    edge = lax.ppermute(edge, "tile", swap)
    sent = call(
        second_source_kernel, "v" * 11, "v", f32(NX * SENT, LANES), [pltpu.VMEM((NCOMP, LANES), jnp.float32)]
    )(moved, one, two, edge, spectrum, coef, spread, vec, stress, owner, cell)
    arrived = lax.all_to_all(sent.reshape(NX * SENT, 1, LANES), "comp", split_axis=0, concat_axis=0, tiled=True)
    arrived = arrived.reshape(NX * SENT, LANES)
    mine = call(edges_kernel, "v", "v", f32(NX + 8, LANES))(arrived)
    theirs = lax.ppermute(mine, "tile", swap)
    adjoint, gradient = call(
        last_kernel, "vvvv", "hv", (f32(LOCAL, NX, LANES), f32(NSTEP, CELLS // 2)), held
    )(arrived, mine, theirs, face)
    return adjoint, gradient.T


def solution(mesh):
    in_specs = (
        P("comp", None, "tile"),
        P(None, None, "comp", "tile"),
        P(None, "comp", "tile"),
        P(None, "comp", "tile"),
        P(None, "comp", "tile"),
        P(),
        P(),
        P(),
        P(),
        P(None, "comp", "tile"),
        P(None, "comp", "tile"),
    )
    out_specs = (P("comp", None, "tile"), P(("comp", "tile"), None))
    return jax.shard_map(shards, mesh=mesh, in_specs=in_specs, out_specs=out_specs, check_vma=False)
```

```python
import math

import jax
import jax.numpy as jnp
import numpy as np
from jax import lax
from jax.experimental import pallas as pl
from jax.experimental.pallas import tpu as pltpu
from jax.sharding import PartitionSpec as P

NDIR = 36
NFREQ = 32
NSTEP = 2
NCOMP = NDIR * NFREQ
NX = 128
LANES = 128
LOCAL = 9
QUART = 4
SENT = LOCAL + 1
CELLS = 16

THETA = np.arange(NDIR) * (2.0 * math.pi / NDIR)
COS = [0.0 if d % 18 == 9 else math.cos(t) for d, t in enumerate(THETA)]
SIN = [0.0 if d % 18 == 0 else math.sin(t) for d, t in enumerate(THETA)]
EAST = list(range(27, NDIR)) + list(range(0, 9))
WEST = list(range(9, 27))
assert all(COS[d] >= 0 for d in EAST) and all(COS[d] <= 0 for d in WEST)
assert all(SIN[d] >= 0 for d in range(18)) and all(SIN[d] <= 0 for d in range(18, 36))
ORDER = EAST + WEST
PLACE = {d: p for p, d in enumerate(ORDER)}
HALF = len(EAST) * NFREQ

GROWTH, DISSIP, KEEP, TURN_NEG, TURN_POS, UP, DOWN, RIGHT, LEFT, GAIN0, GAIN1, LOSS0, LOSS1 = range(13)
GAIN, LOSS = (GAIN0, GAIN1), (LOSS0, LOSS1)
PART = NSTEP * CELLS

PARAMS = pltpu.CompilerParams(vmem_limit_bytes=24 * 1024 * 1024)
WHOLE = pltpu.CompilerParams(vmem_limit_bytes=60 * 1024 * 1024)


def lane_iota(rows):
    return lax.broadcasted_iota(jnp.int32, (rows, LANES), 1)


def sub_iota(rows):
    return lax.broadcasted_iota(jnp.int32, (rows, LANES), 0)


def by_row_kernel(in_ref, out_ref, held_ref, sems):
    copies = [pltpu.make_async_copy(in_ref.at[j], held_ref.at[j], sems.at[j]) for j in range(LOCAL)]
    for copy in copies:
        copy.start()
    for j, copy in enumerate(copies):
        copy.wait()
        out_ref[pl.ds(j, NX, stride=LOCAL), :] = held_ref[j]


def prepare_kernel(
    spectrum_ref, friction_ref, wind_ref, refraction_ref, courant_ref, growth_ref, dissip_ref, mask_ref,
    index_ref, weight_ref, coef_ref, spread_ref, vec_ref, face_ref, owner_ref, cell_ref,
):
    row = lax.axis_index("comp")
    tile = lax.axis_index("tile")
    left_half = mask_ref[:, :LANES].astype(jnp.float32)
    right_half = mask_ref[:, LANES:].astype(jnp.float32)
    first = tile == 0
    own = jnp.where(first, left_half, right_half)
    lane = lane_iota(NX)
    sub = sub_iota(NX)
    other = jnp.where(first, right_half, left_half)
    nxt = jnp.where(lane == LANES - 1, jnp.where(first, pltpu.roll(other, LANES - 1, 1), 0.0), pltpu.roll(own, LANES - 1, 1))
    prv = jnp.where(lane == 0, jnp.where(first, 0.0, pltpu.roll(other, 1, 1)), pltpu.roll(own, 1, 1))
    quarter = row % QUART
    speed = courant_ref[row // QUART]
    up = own * jnp.where(sub == NX - 1, 0.0, pltpu.roll(own, NX - 1, 0))
    down = own * jnp.where(sub == 0, 0.0, pltpu.roll(own, 1, 0))
    right, left = own * nxt, own * prv
    face_ref[0] = speed * jnp.where((quarter == 0) | (quarter == 3), up, down)
    face_ref[1] = speed * jnp.where(quarter < 2, right, left)
    pick = sub == row
    mask, *faces = [
        jnp.sum(jnp.where(pick, value, 0.0), axis=0, keepdims=True) for value in (own, up, down, right, left)
    ]

    sub_f = sub_iota(NFREQ)
    growth = jnp.zeros((NFREQ, LANES), jnp.float32)
    dissip = jnp.zeros((NFREQ, LANES), jnp.float32)
    courant = jnp.zeros((NFREQ, LANES), jnp.float32)
    for f in range(NFREQ):
        at = sub_f == f
        growth = jnp.where(at, growth_ref[f], growth)
        dissip = jnp.where(at, dissip_ref[f], dissip)
        courant = jnp.where(at, courant_ref[f], courant)
    turn = refraction_ref[...]
    coef_ref[GROWTH] = growth
    coef_ref[DISSIP] = dissip
    coef_ref[KEEP] = 1.0 - jnp.abs(turn)
    coef_ref[TURN_NEG] = jnp.minimum(turn, 0.0)
    coef_ref[TURN_POS] = jnp.maximum(turn, 0.0)
    for k, name in enumerate((UP, DOWN, RIGHT, LEFT)):
        coef_ref[name] = courant * faces[k]
    vec_ref[...] = jnp.zeros_like(vec_ref)
    vec_ref[2:3] = mask
    theta = sub_iota(NDIR).astype(jnp.float32) * (2.0 * math.pi / NDIR)
    for n in range(NSTEP):
        total = jnp.zeros((8, LANES), jnp.float32)
        for k in range(NCOMP // 8):
            total = total + spectrum_ref[n, pl.ds(8 * k, 8), :]
        energy = jnp.sum(total, axis=0, keepdims=True) / NFREQ
        vec_ref[n : n + 1] = (2.0 / NFREQ) * energy * mask
        coef_ref[GAIN[n]] = growth * (friction_ref[n : n + 1] * mask)
        coef_ref[LOSS[n]] = mask - dissip * (energy * energy * mask)
        spread_ref[n] = jnp.maximum(jnp.cos(theta - wind_ref[n : n + 1]), 0.0)

    sub_c = sub_iota(PART)
    for corner in range(4):
        lanes = slice(corner * LANES, (corner + 1) * LANES)
        index = index_ref[corner : corner + 1, :]
        owner_ref[:, lanes] = jnp.where(sub == index // CELLS, 1.0, 0.0).astype(jnp.bfloat16)
        cell_ref[:, lanes] = jnp.where(sub_c % CELLS == index % CELLS, weight_ref[corner : corner + 1, :], 0.0)


def source_sums(adjoint_of, spectrum_ref, coef_ref, spread_ref, vec_ref, step):
    damped = jnp.zeros((8, LANES), jnp.float32)
    stress = jnp.zeros((8, LANES), jnp.float32)
    for b in range(NFREQ // 8):
        plain = jnp.zeros((8, LANES), jnp.float32)
        spread = jnp.zeros((8, LANES), jnp.float32)
        for p, d in enumerate(ORDER):
            product = spectrum_ref[step, pl.ds(8 * b * NDIR + d, 8, stride=NDIR), :] * adjoint_of(b, p, d)
            plain = plain + product
            spread = spread + spread_ref[step, d : d + 1, :] * product
        damped = damped + coef_ref[DISSIP, 8 * b : 8 * b + 8] * plain
        stress = stress + coef_ref[GROWTH, 8 * b : 8 * b + 8] * spread
    damped = jnp.sum(damped, axis=0, keepdims=True)
    stress = jnp.sum(stress, axis=0, keepdims=True)
    return vec_ref[step : step + 1] * damped, vec_ref[2:3] * stress


def source_update(adjoint_of, store, coef_ref, spread_ref, shared, step):
    shared = jnp.broadcast_to(shared, (8, LANES))
    for b in range(NFREQ // 8):
        rows = slice(8 * b, 8 * b + 8)
        gain, loss = coef_ref[GAIN[step], rows], coef_ref[LOSS[step], rows]
        keep, neg, pos = coef_ref[KEEP, rows], coef_ref[TURN_NEG, rows], coef_ref[TURN_POS, rows]

        def updated(d):
            return adjoint_of(b, PLACE[d], d) * (loss + gain * spread_ref[step, d : d + 1, :]) - shared

        before, here, first = updated(ORDER[-1]), updated(ORDER[0]), None
        first = here
        for p, d in enumerate(ORDER):
            after = updated(ORDER[p + 1]) if p + 1 < NDIR else first
            store(b, p, d, keep * here - neg * before + pos * after)
            before, here = here, after


def first_source_kernel(
    adjoint_ref, spectrum_ref, coef_ref, spread_ref, vec_ref, moved_ref, one_ref, two_ref, edge_ref, stress_ref
):
    step = NSTEP - 1

    def adjoint_of(b, p, d):
        return adjoint_ref[pl.ds(8 * b * NDIR + d, 8, stride=NDIR), :]

    shared, stress = source_sums(adjoint_of, spectrum_ref, coef_ref, spread_ref, vec_ref, step)
    stress_ref[...] = jnp.broadcast_to(stress, (8, LANES))
    lane = lane_iota(8)
    edges = [jnp.zeros((8, LANES), jnp.float32) for _ in range(NFREQ // 8)]

    def store(b, p, d, value):
        moved_ref[pl.ds(p * NFREQ + 8 * b, 8), :] = value
        column = value[:, :1] if SIN[d] >= 0 else value[:, LANES - 1 :]
        edges[b] = jnp.where(lane == p, column, edges[b])

    source_update(adjoint_of, store, coef_ref, spread_ref, shared, step)
    for b in range(NFREQ // 8):
        edge_ref[8 * b : 8 * b + 8] = edges[b]
    odd = lax.axis_index("comp") % 2

    @pl.when(odd == 1)
    def _():
        one_ref[...] = moved_ref[:HALF]
        two_ref[...] = moved_ref[HALF:]

    @pl.when(odd == 0)
    def _():
        one_ref[...] = moved_ref[HALF:]
        two_ref[...] = moved_ref[:HALF]


def second_source_kernel(
    moved_ref, one_ref, two_ref, edge_ref, spectrum_ref, coef_ref, spread_ref, vec_ref, stress_ref,
    owner_ref, cell_ref, out_ref, held_ref,
):
    step = 0
    lane = lane_iota(8)
    even = jnp.broadcast_to(lax.axis_index("comp") % 2, (8, LANES)) == 0

    def propagated(b, p, d):
        rows = slice(8 * b, 8 * b + 8)
        east = p < NDIR // 2
        face, at = (UP, p) if east else (DOWN, p - NDIR // 2)
        centre = moved_ref[pl.ds(p * NFREQ + 8 * b, 8), :]
        one = one_ref[pl.ds(at * NFREQ + 8 * b, 8), :]
        two = two_ref[pl.ds(at * NFREQ + 8 * b, 8), :]
        row = jnp.where(even, one, two) if east else jnp.where(even, two, one)
        arrived = edge_ref[rows, p : p + 1]
        if SIN[d] >= 0:
            side, column = RIGHT, jnp.where(lane == LANES - 1, arrived, pltpu.roll(centre, LANES - 1, 1))
        else:
            side, column = LEFT, jnp.where(lane == 0, arrived, pltpu.roll(centre, 1, 1))
        value = (
            centre
            + abs(COS[d]) * (coef_ref[face, rows] * (row - centre))
            + abs(SIN[d]) * (coef_ref[side, rows] * (column - centre))
        )
        held_ref[pl.ds(p * NFREQ + 8 * b, 8), :] = value
        return value

    shared, stress = source_sums(propagated, spectrum_ref, coef_ref, spread_ref, vec_ref, step)

    values = jnp.concatenate(
        [
            cell_ref[CELLS * n : CELLS * n + CELLS, :] * jnp.concatenate([row] * 4, axis=1)
            for n, row in enumerate((stress, stress_ref[:1]))
        ],
        axis=0,
    )
    parts = []
    for _ in range(3):
        parts.append(values.astype(jnp.bfloat16))
        values = values - parts[-1].astype(jnp.float32)
    parts.append(jnp.zeros_like(parts[0]))
    cells = lax.dot_general(
        owner_ref[...], jnp.concatenate(parts, axis=0), (((1,), (1,)), ((), ())), preferred_element_type=jnp.float32
    )
    out_ref[pl.ds(LOCAL, NX, stride=SENT), :] = cells

    def adjoint_of(b, p, d):
        return held_ref[pl.ds(p * NFREQ + 8 * b, 8), :]

    def store(b, p, d, value):
        at = 8 * b * QUART * SENT + d // LOCAL * SENT + d % LOCAL
        out_ref[pl.ds(at, 8, stride=QUART * SENT), :] = value

    source_update(adjoint_of, store, coef_ref, spread_ref, shared, step)


def edges_kernel(arrived_ref, out_ref):
    lane = lane_iota(NX)
    quarter = lax.axis_index("comp") % QUART
    for north in (True, False):

        @pl.when((quarter < 2) == north)
        def _():
            edges = jnp.zeros((NX, LANES), jnp.float32)
            for j in range(LOCAL):
                value = arrived_ref[pl.ds(j, NX, stride=SENT), :]
                edges = jnp.where(lane == j, value[:, :1] if north else value[:, LANES - 1 :], edges)
            out_ref[:NX] = edges

    cells = arrived_ref[pl.ds(LOCAL, NX, stride=SENT), :]
    out_ref[NX:] = jnp.broadcast_to(jnp.sum(cells, axis=0, keepdims=True), (8, LANES))


def last_kernel(arrived_ref, mine_ref, edges_ref, face_ref, adjoint_ref, gradient_ref, held_ref, sems):
    tile = lax.axis_index("tile")
    quarter = lax.axis_index("comp") % QUART
    lane = lane_iota(NX)
    copies = [pltpu.make_async_copy(held_ref.at[j], adjoint_ref.at[j], sems.at[j]) for j in range(LOCAL)]
    for q in range(QUART):

        @pl.when(quarter == q)
        def _():
            for j in range(LOCAL):
                d = q * LOCAL + j
                centre = arrived_ref[pl.ds(j, NX, stride=SENT), :]
                arrived = edges_ref[:NX, j : j + 1]
                row = pltpu.roll(centre, NX - 1 if d in EAST else 1, 0)
                if SIN[q * LOCAL + 1] > 0:
                    column = jnp.where(lane == LANES - 1, arrived, pltpu.roll(centre, LANES - 1, 1))
                else:
                    column = jnp.where(lane == 0, arrived, pltpu.roll(centre, 1, 1))
                held_ref[j] = (
                    centre
                    + abs(COS[d]) * (face_ref[0] * (row - centre))
                    + abs(SIN[d]) * (face_ref[1] * (column - centre))
                )
                copies[j].start()

    cells = mine_ref[NX:] + edges_ref[NX:]
    cells = cells + pltpu.roll(cells, LANES - PART, 1) + pltpu.roll(cells, LANES - 2 * PART, 1)
    for n in range(NSTEP):
        at = pltpu.roll(cells, LANES - n * CELLS - tile * (CELLS // 2), 1)
        gradient_ref[n : n + 1, :] = at[:1, : CELLS // 2]
    for copy in copies:
        copy.wait()


def f32(*shape):
    return jax.ShapeDtypeStruct(shape, jnp.float32)


SPACES = {"s": pltpu.SMEM, "v": pltpu.VMEM, "h": pltpu.HBM}


def spec(spaces):
    return [pl.BlockSpec(memory_space=SPACES[space]) for space in spaces]


def call(kernel, inputs, outputs, out_shape, scratch=(), params=PARAMS):
    single = len(outputs) == 1
    return pl.pallas_call(
        kernel,
        in_specs=spec(inputs),
        out_specs=spec(outputs)[0] if single else tuple(spec(outputs)),
        out_shape=out_shape,
        scratch_shapes=list(scratch),
        compiler_params=params,
    )


def shards(
    adjoint_final,
    background,
    friction_velocity,
    wind_direction,
    refraction_rate,
    courant,
    growth_rate,
    dissipation_rate,
    sea_mask,
    interp_index,
    interp_weight,
):
    comp_count = lax.axis_size("comp")
    spectrum = background.reshape(NSTEP, NCOMP, LANES)
    held = [pltpu.VMEM((LOCAL, NX, LANES), jnp.float32), pltpu.SemaphoreType.DMA((LOCAL,))]
    by_row = call(by_row_kernel, "h", "v", f32(NCOMP, LANES), held, WHOLE)(adjoint_final)
    points = lax.all_to_all(by_row.reshape(NCOMP, 1, LANES), "comp", split_axis=0, concat_axis=0, tiled=True)
    points = points.reshape(NCOMP, LANES)
    coef, spread, vec, face, owner, cell = call(
        prepare_kernel,
        "vvvvsssvvv",
        "vvvvvv",
        (
            f32(13, NFREQ, LANES),
            f32(NSTEP, NDIR, LANES),
            f32(8, LANES),
            f32(2, NX, LANES),
            jax.ShapeDtypeStruct((NX, 4 * LANES), jnp.bfloat16),
            f32(PART, 4 * LANES),
        ),
    )(
        spectrum,
        friction_velocity.reshape(NSTEP, LANES),
        wind_direction.reshape(NSTEP, LANES),
        refraction_rate.reshape(NFREQ, LANES),
        courant,
        growth_rate,
        dissipation_rate,
        sea_mask,
        interp_index.reshape(4, LANES),
        interp_weight.reshape(4, LANES),
    )
    moved, one, two, edge, stress = call(
        first_source_kernel,
        "vvvvv",
        "vvvvv",
        (f32(NCOMP, LANES), f32(HALF, LANES), f32(HALF, LANES), f32(NFREQ, LANES), f32(8, LANES)),
    )(points, spectrum, coef, spread, vec)
    swap = [(0, 1), (1, 0)]
    one = lax.ppermute(one, "comp", [(i, i ^ 1) for i in range(comp_count)])
    two = lax.ppermute(two, "comp", [(i, ((i + 1) ^ 1) - 1) for i in range(1, comp_count - 1)])
    edge = lax.ppermute(edge, "tile", swap)
    sent = call(
        second_source_kernel, "v" * 11, "v", f32(NX * SENT, LANES), [pltpu.VMEM((NCOMP, LANES), jnp.float32)]
    )(moved, one, two, edge, spectrum, coef, spread, vec, stress, owner, cell)
    arrived = lax.all_to_all(sent.reshape(NX * SENT, 1, LANES), "comp", split_axis=0, concat_axis=0, tiled=True)
    arrived = arrived.reshape(NX * SENT, LANES)
    mine = call(edges_kernel, "v", "v", f32(NX + 8, LANES))(arrived)
    theirs = lax.ppermute(mine, "tile", swap)
    adjoint, gradient = call(
        last_kernel, "vvvv", "hv", (f32(LOCAL, NX, LANES), f32(NSTEP, CELLS // 2)), held
    )(arrived, mine, theirs, face)
    return adjoint, gradient.T


def solution(mesh):
    in_specs = (
        P("comp", None, "tile"),
        P(None, None, "comp", "tile"),
        P(None, "comp", "tile"),
        P(None, "comp", "tile"),
        P(None, "comp", "tile"),
        P(),
        P(),
        P(),
        P(),
        P(None, "comp", "tile"),
        P(None, "comp", "tile"),
    )
    out_specs = (P("comp", None, "tile"), P(("comp", "tile"), None))
    return jax.shard_map(shards, mesh=mesh, in_specs=in_specs, out_specs=out_specs, check_vma=False)
```

```python
import math

import jax
import jax.numpy as jnp
import numpy as np
from jax import lax
from jax.experimental import pallas as pl
from jax.experimental.pallas import tpu as pltpu
from jax.sharding import PartitionSpec as P

NDIR = 36
NFREQ = 32
NSTEP = 2
NCOMP = NDIR * NFREQ
NX = 128
LANES = 128
LOCAL = 9
QUART = 4
SENT = LOCAL + 1
CHUNKS = 2
CELLS = 16

THETA = np.arange(NDIR) * (2.0 * math.pi / NDIR)
COS = [0.0 if d % 18 == 9 else math.cos(t) for d, t in enumerate(THETA)]
SIN = [0.0 if d % 18 == 0 else math.sin(t) for d, t in enumerate(THETA)]
EAST = list(range(27, NDIR)) + list(range(0, 9))
WEST = list(range(9, 27))
assert all(COS[d] >= 0 for d in EAST) and all(COS[d] <= 0 for d in WEST)
assert all(SIN[d] >= 0 for d in range(18)) and all(SIN[d] <= 0 for d in range(18, 36))
ORDER = EAST + WEST
PLACE = {d: p for p, d in enumerate(ORDER)}
HALF = len(EAST) * NFREQ

GROWTH, DISSIP, KEEP, TURN_NEG, TURN_POS, UP, DOWN, RIGHT, LEFT, GAIN0, GAIN1, LOSS0, LOSS1 = range(13)
GAIN, LOSS = (GAIN0, GAIN1), (LOSS0, LOSS1)
PART = NSTEP * CELLS

PARAMS = pltpu.CompilerParams(vmem_limit_bytes=24 * 1024 * 1024)
WHOLE = pltpu.CompilerParams(vmem_limit_bytes=60 * 1024 * 1024)


def lane_iota(rows):
    return lax.broadcasted_iota(jnp.int32, (rows, LANES), 1)


def sub_iota(rows):
    return lax.broadcasted_iota(jnp.int32, (rows, LANES), 0)


def by_row_kernel(in_ref, out_ref, held_ref, in_sems, rows_ref, out_sems):
    count = NX // CHUNKS
    ins, outs = [], []
    for c in range(CHUNKS):
        part = pl.ds(c * count, count)
        ins.append(pltpu.make_async_copy(in_ref.at[:, part, :], held_ref.at[:, part, :], in_sems.at[c]))
        part = pl.ds(c * count * LOCAL, count * LOCAL)
        outs.append(pltpu.make_async_copy(rows_ref.at[part, :], out_ref.at[part, :], out_sems.at[c]))
        ins[c].start()
    for c in range(CHUNKS):
        ins[c].wait()
        for j in range(LOCAL):
            rows_ref[pl.ds(c * count * LOCAL + j, count, stride=LOCAL), :] = held_ref[j, c * count : (c + 1) * count]
        outs[c].start()
    for copy in outs:
        copy.wait()


def prepare_kernel(
    spectrum_ref, friction_ref, wind_ref, refraction_ref, courant_ref, growth_ref, dissip_ref, mask_ref,
    index_ref, weight_ref, coef_ref, spread_ref, vec_ref, face_ref, owner_ref, cell_ref,
):
    row = lax.axis_index("comp")
    tile = lax.axis_index("tile")
    left_half = mask_ref[:, :LANES].astype(jnp.float32)
    right_half = mask_ref[:, LANES:].astype(jnp.float32)
    first = tile == 0
    own = jnp.where(first, left_half, right_half)
    lane = lane_iota(NX)
    sub = sub_iota(NX)
    other = jnp.where(first, right_half, left_half)
    nxt = jnp.where(lane == LANES - 1, jnp.where(first, pltpu.roll(other, LANES - 1, 1), 0.0), pltpu.roll(own, LANES - 1, 1))
    prv = jnp.where(lane == 0, jnp.where(first, 0.0, pltpu.roll(other, 1, 1)), pltpu.roll(own, 1, 1))
    quarter = row % QUART
    speed = courant_ref[row // QUART]
    up = own * jnp.where(sub == NX - 1, 0.0, pltpu.roll(own, NX - 1, 0))
    down = own * jnp.where(sub == 0, 0.0, pltpu.roll(own, 1, 0))
    right, left = own * nxt, own * prv
    face_ref[0] = speed * jnp.where((quarter == 0) | (quarter == 3), up, down)
    face_ref[1] = speed * jnp.where(quarter < 2, right, left)
    pick = sub == row
    mask, *faces = [
        jnp.sum(jnp.where(pick, value, 0.0), axis=0, keepdims=True) for value in (own, up, down, right, left)
    ]

    sub_f = sub_iota(NFREQ)
    growth = jnp.zeros((NFREQ, LANES), jnp.float32)
    dissip = jnp.zeros((NFREQ, LANES), jnp.float32)
    courant = jnp.zeros((NFREQ, LANES), jnp.float32)
    for f in range(NFREQ):
        at = sub_f == f
        growth = jnp.where(at, growth_ref[f], growth)
        dissip = jnp.where(at, dissip_ref[f], dissip)
        courant = jnp.where(at, courant_ref[f], courant)
    turn = refraction_ref[...]
    coef_ref[GROWTH] = growth
    coef_ref[DISSIP] = dissip
    coef_ref[KEEP] = 1.0 - jnp.abs(turn)
    coef_ref[TURN_NEG] = jnp.minimum(turn, 0.0)
    coef_ref[TURN_POS] = jnp.maximum(turn, 0.0)
    for k, name in enumerate((UP, DOWN, RIGHT, LEFT)):
        coef_ref[name] = courant * faces[k]
    vec_ref[...] = jnp.zeros_like(vec_ref)
    vec_ref[2:3] = mask
    theta = sub_iota(NDIR).astype(jnp.float32) * (2.0 * math.pi / NDIR)
    for n in range(NSTEP):
        total = jnp.zeros((8, LANES), jnp.float32)
        for k in range(NCOMP // 8):
            total = total + spectrum_ref[n, pl.ds(8 * k, 8), :]
        energy = jnp.sum(total, axis=0, keepdims=True) / NFREQ
        vec_ref[n : n + 1] = (2.0 / NFREQ) * energy * mask
        coef_ref[GAIN[n]] = growth * (friction_ref[n : n + 1] * mask)
        coef_ref[LOSS[n]] = mask - dissip * (energy * energy * mask)
        spread_ref[n] = jnp.maximum(jnp.cos(theta - wind_ref[n : n + 1]), 0.0)

    sub_c = sub_iota(PART)
    for corner in range(4):
        lanes = slice(corner * LANES, (corner + 1) * LANES)
        index = index_ref[corner : corner + 1, :]
        owner_ref[:, lanes] = jnp.where(sub == index // CELLS, 1.0, 0.0).astype(jnp.bfloat16)
        cell_ref[:, lanes] = jnp.where(sub_c % CELLS == index % CELLS, weight_ref[corner : corner + 1, :], 0.0)


def source_sums(adjoint_of, spectrum_ref, coef_ref, spread_ref, vec_ref, step):
    damped = jnp.zeros((8, LANES), jnp.float32)
    stress = jnp.zeros((8, LANES), jnp.float32)
    for b in range(NFREQ // 8):
        plain = jnp.zeros((8, LANES), jnp.float32)
        spread = jnp.zeros((8, LANES), jnp.float32)
        for p, d in enumerate(ORDER):
            product = spectrum_ref[step, pl.ds(8 * b * NDIR + d, 8, stride=NDIR), :] * adjoint_of(b, p, d)
            plain = plain + product
            spread = spread + spread_ref[step, d : d + 1, :] * product
        damped = damped + coef_ref[DISSIP, 8 * b : 8 * b + 8] * plain
        stress = stress + coef_ref[GROWTH, 8 * b : 8 * b + 8] * spread
    damped = jnp.sum(damped, axis=0, keepdims=True)
    stress = jnp.sum(stress, axis=0, keepdims=True)
    return vec_ref[step : step + 1] * damped, vec_ref[2:3] * stress


def source_update(adjoint_of, store, coef_ref, spread_ref, shared, step):
    shared = jnp.broadcast_to(shared, (8, LANES))
    for b in range(NFREQ // 8):
        rows = slice(8 * b, 8 * b + 8)
        gain, loss = coef_ref[GAIN[step], rows], coef_ref[LOSS[step], rows]
        keep, neg, pos = coef_ref[KEEP, rows], coef_ref[TURN_NEG, rows], coef_ref[TURN_POS, rows]

        def updated(d):
            return adjoint_of(b, PLACE[d], d) * (loss + gain * spread_ref[step, d : d + 1, :]) - shared

        before, here, first = updated(ORDER[-1]), updated(ORDER[0]), None
        first = here
        for p, d in enumerate(ORDER):
            after = updated(ORDER[p + 1]) if p + 1 < NDIR else first
            store(b, p, d, keep * here - neg * before + pos * after)
            before, here = here, after


def first_source_kernel(
    adjoint_ref, spectrum_ref, coef_ref, spread_ref, vec_ref, moved_ref, one_ref, two_ref, edge_ref, stress_ref
):
    step = NSTEP - 1

    def adjoint_of(b, p, d):
        return adjoint_ref[pl.ds(8 * b * NDIR + d, 8, stride=NDIR), :]

    shared, stress = source_sums(adjoint_of, spectrum_ref, coef_ref, spread_ref, vec_ref, step)
    stress_ref[...] = jnp.broadcast_to(stress, (8, LANES))
    lane = lane_iota(8)
    edges = [jnp.zeros((8, LANES), jnp.float32) for _ in range(NFREQ // 8)]

    def store(b, p, d, value):
        moved_ref[pl.ds(p * NFREQ + 8 * b, 8), :] = value
        column = value[:, :1] if SIN[d] >= 0 else value[:, LANES - 1 :]
        edges[b] = jnp.where(lane == p, column, edges[b])

    source_update(adjoint_of, store, coef_ref, spread_ref, shared, step)
    for b in range(NFREQ // 8):
        edge_ref[8 * b : 8 * b + 8] = edges[b]
    odd = lax.axis_index("comp") % 2

    @pl.when(odd == 1)
    def _():
        one_ref[...] = moved_ref[:HALF]
        two_ref[...] = moved_ref[HALF:]

    @pl.when(odd == 0)
    def _():
        one_ref[...] = moved_ref[HALF:]
        two_ref[...] = moved_ref[:HALF]


def second_source_kernel(
    moved_ref, one_ref, two_ref, edge_ref, spectrum_ref, coef_ref, spread_ref, vec_ref, stress_ref,
    owner_ref, cell_ref, out_ref, held_ref,
):
    step = 0
    lane = lane_iota(8)
    even = jnp.broadcast_to(lax.axis_index("comp") % 2, (8, LANES)) == 0

    def propagated(b, p, d):
        rows = slice(8 * b, 8 * b + 8)
        east = p < NDIR // 2
        face, at = (UP, p) if east else (DOWN, p - NDIR // 2)
        centre = moved_ref[pl.ds(p * NFREQ + 8 * b, 8), :]
        one = one_ref[pl.ds(at * NFREQ + 8 * b, 8), :]
        two = two_ref[pl.ds(at * NFREQ + 8 * b, 8), :]
        row = jnp.where(even, one, two) if east else jnp.where(even, two, one)
        arrived = edge_ref[rows, p : p + 1]
        if SIN[d] >= 0:
            side, column = RIGHT, jnp.where(lane == LANES - 1, arrived, pltpu.roll(centre, LANES - 1, 1))
        else:
            side, column = LEFT, jnp.where(lane == 0, arrived, pltpu.roll(centre, 1, 1))
        value = (
            centre
            + abs(COS[d]) * (coef_ref[face, rows] * (row - centre))
            + abs(SIN[d]) * (coef_ref[side, rows] * (column - centre))
        )
        held_ref[pl.ds(p * NFREQ + 8 * b, 8), :] = value
        return value

    shared, stress = source_sums(propagated, spectrum_ref, coef_ref, spread_ref, vec_ref, step)

    values = jnp.concatenate(
        [
            cell_ref[CELLS * n : CELLS * n + CELLS, :] * jnp.concatenate([row] * 4, axis=1)
            for n, row in enumerate((stress, stress_ref[:1]))
        ],
        axis=0,
    )
    parts = []
    for _ in range(3):
        parts.append(values.astype(jnp.bfloat16))
        values = values - parts[-1].astype(jnp.float32)
    parts.append(jnp.zeros_like(parts[0]))
    cells = lax.dot_general(
        owner_ref[...], jnp.concatenate(parts, axis=0), (((1,), (1,)), ((), ())), preferred_element_type=jnp.float32
    )
    out_ref[pl.ds(LOCAL, NX, stride=SENT), :] = cells

    def adjoint_of(b, p, d):
        return held_ref[pl.ds(p * NFREQ + 8 * b, 8), :]

    def store(b, p, d, value):
        at = 8 * b * QUART * SENT + d // LOCAL * SENT + d % LOCAL
        out_ref[pl.ds(at, 8, stride=QUART * SENT), :] = value

    source_update(adjoint_of, store, coef_ref, spread_ref, shared, step)


def edges_kernel(arrived_ref, out_ref):
    lane = lane_iota(NX)
    quarter = lax.axis_index("comp") % QUART
    for north in (True, False):

        @pl.when((quarter < 2) == north)
        def _():
            edges = jnp.zeros((NX, LANES), jnp.float32)
            for j in range(LOCAL):
                value = arrived_ref[pl.ds(j, NX, stride=SENT), :]
                edges = jnp.where(lane == j, value[:, :1] if north else value[:, LANES - 1 :], edges)
            out_ref[:NX] = edges

    cells = arrived_ref[pl.ds(LOCAL, NX, stride=SENT), :]
    out_ref[NX:] = jnp.broadcast_to(jnp.sum(cells, axis=0, keepdims=True), (8, LANES))


def last_kernel(arrived_ref, mine_ref, edges_ref, face_ref, adjoint_ref, gradient_ref, held_ref, sems):
    tile = lax.axis_index("tile")
    quarter = lax.axis_index("comp") % QUART
    lane = lane_iota(NX)
    copies = [pltpu.make_async_copy(held_ref.at[j], adjoint_ref.at[j], sems.at[j]) for j in range(LOCAL)]
    for q in range(QUART):

        @pl.when(quarter == q)
        def _():
            for j in range(LOCAL):
                d = q * LOCAL + j
                centre = arrived_ref[pl.ds(j, NX, stride=SENT), :]
                arrived = edges_ref[:NX, j : j + 1]
                row = pltpu.roll(centre, NX - 1 if d in EAST else 1, 0)
                if SIN[q * LOCAL + 1] > 0:
                    column = jnp.where(lane == LANES - 1, arrived, pltpu.roll(centre, LANES - 1, 1))
                else:
                    column = jnp.where(lane == 0, arrived, pltpu.roll(centre, 1, 1))
                held_ref[j] = (
                    centre
                    + abs(COS[d]) * (face_ref[0] * (row - centre))
                    + abs(SIN[d]) * (face_ref[1] * (column - centre))
                )
                copies[j].start()

    cells = mine_ref[NX:] + edges_ref[NX:]
    cells = cells + pltpu.roll(cells, LANES - PART, 1) + pltpu.roll(cells, LANES - 2 * PART, 1)
    for n in range(NSTEP):
        at = pltpu.roll(cells, LANES - n * CELLS - tile * (CELLS // 2), 1)
        gradient_ref[n : n + 1, :] = at[:1, : CELLS // 2]
    for copy in copies:
        copy.wait()


def f32(*shape):
    return jax.ShapeDtypeStruct(shape, jnp.float32)


SPACES = {"s": pltpu.SMEM, "v": pltpu.VMEM, "h": pltpu.HBM}


def spec(spaces):
    return [pl.BlockSpec(memory_space=SPACES[space]) for space in spaces]


def call(kernel, inputs, outputs, out_shape, scratch=(), params=PARAMS):
    single = len(outputs) == 1
    return pl.pallas_call(
        kernel,
        in_specs=spec(inputs),
        out_specs=spec(outputs)[0] if single else tuple(spec(outputs)),
        out_shape=out_shape,
        scratch_shapes=list(scratch),
        compiler_params=params,
    )


def shards(
    adjoint_final,
    background,
    friction_velocity,
    wind_direction,
    refraction_rate,
    courant,
    growth_rate,
    dissipation_rate,
    sea_mask,
    interp_index,
    interp_weight,
):
    comp_count = lax.axis_size("comp")
    spectrum = background.reshape(NSTEP, NCOMP, LANES)
    held = [pltpu.VMEM((LOCAL, NX, LANES), jnp.float32), pltpu.SemaphoreType.DMA((LOCAL,))]
    sems = pltpu.SemaphoreType.DMA((CHUNKS,))
    by_row = call(
        by_row_kernel, "h", "h", f32(NCOMP, LANES), [held[0], sems, pltpu.VMEM((NCOMP, LANES), jnp.float32), sems], WHOLE
    )(adjoint_final)
    points = lax.all_to_all(by_row.reshape(NCOMP, 1, LANES), "comp", split_axis=0, concat_axis=0, tiled=True)
    points = points.reshape(NCOMP, LANES)
    coef, spread, vec, face, owner, cell = call(
        prepare_kernel,
        "vvvvsssvvv",
        "vvvvvv",
        (
            f32(13, NFREQ, LANES),
            f32(NSTEP, NDIR, LANES),
            f32(8, LANES),
            f32(2, NX, LANES),
            jax.ShapeDtypeStruct((NX, 4 * LANES), jnp.bfloat16),
            f32(PART, 4 * LANES),
        ),
    )(
        spectrum,
        friction_velocity.reshape(NSTEP, LANES),
        wind_direction.reshape(NSTEP, LANES),
        refraction_rate.reshape(NFREQ, LANES),
        courant,
        growth_rate,
        dissipation_rate,
        sea_mask,
        interp_index.reshape(4, LANES),
        interp_weight.reshape(4, LANES),
    )
    moved, one, two, edge, stress = call(
        first_source_kernel,
        "vvvvv",
        "vvvvv",
        (f32(NCOMP, LANES), f32(HALF, LANES), f32(HALF, LANES), f32(NFREQ, LANES), f32(8, LANES)),
    )(points, spectrum, coef, spread, vec)
    swap = [(0, 1), (1, 0)]
    one = lax.ppermute(one, "comp", [(i, i ^ 1) for i in range(comp_count)])
    two = lax.ppermute(two, "comp", [(i, (((i + 1) ^ 1) - 1) % comp_count) for i in range(comp_count)])
    edge = lax.ppermute(edge, "tile", swap)
    sent = call(
        second_source_kernel, "v" * 11, "v", f32(NX * SENT, LANES), [pltpu.VMEM((NCOMP, LANES), jnp.float32)]
    )(moved, one, two, edge, spectrum, coef, spread, vec, stress, owner, cell)
    arrived = lax.all_to_all(sent.reshape(NX * SENT, 1, LANES), "comp", split_axis=0, concat_axis=0, tiled=True)
    arrived = arrived.reshape(NX * SENT, LANES)
    mine = call(edges_kernel, "v", "v", f32(NX + 8, LANES))(arrived)
    theirs = lax.ppermute(mine, "tile", swap)
    adjoint, gradient = call(
        last_kernel, "vvvv", "hv", (f32(LOCAL, NX, LANES), f32(NSTEP, CELLS // 2)), held
    )(arrived, mine, theirs, face)
    return adjoint, gradient.T


def solution(mesh):
    in_specs = (
        P("comp", None, "tile"),
        P(None, None, "comp", "tile"),
        P(None, "comp", "tile"),
        P(None, "comp", "tile"),
        P(None, "comp", "tile"),
        P(),
        P(),
        P(),
        P(),
        P(None, "comp", "tile"),
        P(None, "comp", "tile"),
    )
    out_specs = (P("comp", None, "tile"), P(("comp", "tile"), None))
    return jax.shard_map(shards, mesh=mesh, in_specs=in_specs, out_specs=out_specs, check_vma=False)
```

```python
import math

import jax
import jax.numpy as jnp
import numpy as np
from jax import lax
from jax.experimental import pallas as pl
from jax.experimental.pallas import tpu as pltpu
from jax.sharding import PartitionSpec as P

NDIR = 36
NFREQ = 32
NSTEP = 2
NCOMP = NDIR * NFREQ
NX = 128
LANES = 128
LOCAL = 9
QUART = 4
SENT = LOCAL + 1
CHUNKS = 2
CELLS = 16

THETA = np.arange(NDIR) * (2.0 * math.pi / NDIR)
COS = [0.0 if d % 18 == 9 else math.cos(t) for d, t in enumerate(THETA)]
SIN = [0.0 if d % 18 == 0 else math.sin(t) for d, t in enumerate(THETA)]
EAST = list(range(27, NDIR)) + list(range(0, 9))
WEST = list(range(9, 27))
assert all(COS[d] >= 0 for d in EAST) and all(COS[d] <= 0 for d in WEST)
assert all(SIN[d] >= 0 for d in range(18)) and all(SIN[d] <= 0 for d in range(18, 36))
ORDER = EAST + WEST
PLACE = {d: p for p, d in enumerate(ORDER)}
HALF = len(EAST) * NFREQ

GROWTH, DISSIP, KEEP, TURN_NEG, TURN_POS, UP, DOWN, RIGHT, LEFT, GAIN0, GAIN1, LOSS0, LOSS1 = range(13)
GAIN, LOSS = (GAIN0, GAIN1), (LOSS0, LOSS1)
PART = NSTEP * CELLS

PARAMS = pltpu.CompilerParams(vmem_limit_bytes=24 * 1024 * 1024)
WHOLE = pltpu.CompilerParams(vmem_limit_bytes=60 * 1024 * 1024)


def lane_iota(rows):
    return lax.broadcasted_iota(jnp.int32, (rows, LANES), 1)


def sub_iota(rows):
    return lax.broadcasted_iota(jnp.int32, (rows, LANES), 0)


def by_row_kernel(in_ref, out_ref, held_ref, in_sems, rows_ref, out_sems):
    count = NX // CHUNKS
    ins, outs = [], []
    for c in range(CHUNKS):
        part = pl.ds(c * count, count)
        ins.append(pltpu.make_async_copy(in_ref.at[:, part, :], held_ref.at[:, part, :], in_sems.at[c]))
        part = pl.ds(c * count * LOCAL, count * LOCAL)
        outs.append(pltpu.make_async_copy(rows_ref.at[part, :], out_ref.at[part, :], out_sems.at[c]))
        ins[c].start()
    for c in range(CHUNKS):
        ins[c].wait()
        for j in range(LOCAL):
            rows_ref[pl.ds(c * count * LOCAL + j, count, stride=LOCAL), :] = held_ref[j, c * count : (c + 1) * count]
        outs[c].start()
    for copy in outs:
        copy.wait()


def prepare_kernel(
    spectrum_ref, friction_ref, wind_ref, refraction_ref, courant_ref, growth_ref, dissip_ref, mask_ref,
    index_ref, weight_ref, coef_ref, spread_ref, vec_ref, face_ref, owner_ref, cell_ref,
):
    row = lax.axis_index("comp")
    tile = lax.axis_index("tile")
    left_half = mask_ref[:, :LANES].astype(jnp.float32)
    right_half = mask_ref[:, LANES:].astype(jnp.float32)
    first = tile == 0
    own = jnp.where(first, left_half, right_half)
    lane = lane_iota(NX)
    sub = sub_iota(NX)
    other = jnp.where(first, right_half, left_half)
    nxt = jnp.where(lane == LANES - 1, jnp.where(first, pltpu.roll(other, LANES - 1, 1), 0.0), pltpu.roll(own, LANES - 1, 1))
    prv = jnp.where(lane == 0, jnp.where(first, 0.0, pltpu.roll(other, 1, 1)), pltpu.roll(own, 1, 1))
    quarter = row % QUART
    speed = courant_ref[row // QUART]
    up = own * jnp.where(sub == NX - 1, 0.0, pltpu.roll(own, NX - 1, 0))
    down = own * jnp.where(sub == 0, 0.0, pltpu.roll(own, 1, 0))
    right, left = own * nxt, own * prv
    face_ref[0] = speed * jnp.where((quarter == 0) | (quarter == 3), up, down)
    face_ref[1] = speed * jnp.where(quarter < 2, right, left)
    pick = sub == row
    mask, *faces = [
        jnp.sum(jnp.where(pick, value, 0.0), axis=0, keepdims=True) for value in (own, up, down, right, left)
    ]

    sub_f = sub_iota(NFREQ)
    growth = jnp.zeros((NFREQ, LANES), jnp.float32)
    dissip = jnp.zeros((NFREQ, LANES), jnp.float32)
    courant = jnp.zeros((NFREQ, LANES), jnp.float32)
    for f in range(NFREQ):
        at = sub_f == f
        growth = jnp.where(at, growth_ref[f], growth)
        dissip = jnp.where(at, dissip_ref[f], dissip)
        courant = jnp.where(at, courant_ref[f], courant)
    turn = refraction_ref[...]
    coef_ref[GROWTH] = growth
    coef_ref[DISSIP] = dissip
    coef_ref[KEEP] = 1.0 - jnp.abs(turn)
    coef_ref[TURN_NEG] = jnp.minimum(turn, 0.0)
    coef_ref[TURN_POS] = jnp.maximum(turn, 0.0)
    for k, name in enumerate((UP, DOWN, RIGHT, LEFT)):
        coef_ref[name] = courant * faces[k]
    vec_ref[...] = jnp.zeros_like(vec_ref)
    vec_ref[2:3] = mask
    theta = sub_iota(NDIR).astype(jnp.float32) * (2.0 * math.pi / NDIR)
    for n in range(NSTEP):
        total = jnp.zeros((8, LANES), jnp.float32)
        for k in range(NCOMP // 8):
            total = total + spectrum_ref[n, pl.ds(8 * k, 8), :]
        energy = jnp.sum(total, axis=0, keepdims=True) / NFREQ
        vec_ref[n : n + 1] = (2.0 / NFREQ) * energy * mask
        coef_ref[GAIN[n]] = growth * (friction_ref[n : n + 1] * mask)
        coef_ref[LOSS[n]] = mask - dissip * (energy * energy * mask)
        spread_ref[n] = jnp.maximum(jnp.cos(theta - wind_ref[n : n + 1]), 0.0)

    sub_c = sub_iota(PART)
    for corner in range(4):
        lanes = slice(corner * LANES, (corner + 1) * LANES)
        index = index_ref[corner : corner + 1, :]
        owner_ref[:, lanes] = jnp.where(sub == index // CELLS, 1.0, 0.0).astype(jnp.bfloat16)
        cell_ref[:, lanes] = jnp.where(sub_c % CELLS == index % CELLS, weight_ref[corner : corner + 1, :], 0.0)


def source_sums(adjoint_of, spectrum_ref, coef_ref, spread_ref, vec_ref, step):
    damped = jnp.zeros((8, LANES), jnp.float32)
    stress = jnp.zeros((8, LANES), jnp.float32)
    for b in range(NFREQ // 8):
        plain = jnp.zeros((8, LANES), jnp.float32)
        spread = jnp.zeros((8, LANES), jnp.float32)
        for p, d in enumerate(ORDER):
            product = spectrum_ref[step, pl.ds(8 * b * NDIR + d, 8, stride=NDIR), :] * adjoint_of(b, p, d)
            plain = plain + product
            spread = spread + spread_ref[step, d : d + 1, :] * product
        damped = damped + coef_ref[DISSIP, 8 * b : 8 * b + 8] * plain
        stress = stress + coef_ref[GROWTH, 8 * b : 8 * b + 8] * spread
    damped = jnp.sum(damped, axis=0, keepdims=True)
    stress = jnp.sum(stress, axis=0, keepdims=True)
    return vec_ref[step : step + 1] * damped, vec_ref[2:3] * stress


def source_update(adjoint_of, store, coef_ref, spread_ref, shared, step):
    shared = jnp.broadcast_to(shared, (8, LANES))
    for b in range(NFREQ // 8):
        rows = slice(8 * b, 8 * b + 8)
        gain, loss = coef_ref[GAIN[step], rows], coef_ref[LOSS[step], rows]
        keep, neg, pos = coef_ref[KEEP, rows], coef_ref[TURN_NEG, rows], coef_ref[TURN_POS, rows]

        def updated(d):
            return adjoint_of(b, PLACE[d], d) * (loss + gain * spread_ref[step, d : d + 1, :]) - shared

        before, here, first = updated(ORDER[-1]), updated(ORDER[0]), None
        first = here
        for p, d in enumerate(ORDER):
            after = updated(ORDER[p + 1]) if p + 1 < NDIR else first
            store(b, p, d, keep * here - neg * before + pos * after)
            before, here = here, after


def first_source_kernel(
    adjoint_ref, spectrum_ref, coef_ref, spread_ref, vec_ref, moved_ref, one_ref, two_ref, edge_ref, stress_ref
):
    step = NSTEP - 1

    def adjoint_of(b, p, d):
        return adjoint_ref[pl.ds(8 * b * NDIR + d, 8, stride=NDIR), :]

    shared, stress = source_sums(adjoint_of, spectrum_ref, coef_ref, spread_ref, vec_ref, step)
    stress_ref[...] = jnp.broadcast_to(stress, (8, LANES))
    lane = lane_iota(8)
    edges = [jnp.zeros((8, LANES), jnp.float32) for _ in range(NFREQ // 8)]

    def store(b, p, d, value):
        moved_ref[pl.ds(p * NFREQ + 8 * b, 8), :] = value
        column = value[:, :1] if SIN[d] >= 0 else value[:, LANES - 1 :]
        edges[b] = jnp.where(lane == p, column, edges[b])

    source_update(adjoint_of, store, coef_ref, spread_ref, shared, step)
    for b in range(NFREQ // 8):
        edge_ref[8 * b : 8 * b + 8] = edges[b]
    odd = lax.axis_index("comp") % 2

    @pl.when(odd == 1)
    def _():
        one_ref[...] = moved_ref[:HALF]
        two_ref[...] = moved_ref[HALF:]

    @pl.when(odd == 0)
    def _():
        one_ref[...] = moved_ref[HALF:]
        two_ref[...] = moved_ref[:HALF]


def second_source_kernel(
    moved_ref, one_ref, two_ref, edge_ref, spectrum_ref, coef_ref, spread_ref, vec_ref, stress_ref,
    owner_ref, cell_ref, out_ref, held_ref,
):
    step = 0
    lane = lane_iota(8)
    even = jnp.broadcast_to(lax.axis_index("comp") % 2, (8, LANES)) == 0

    def propagated(b, p, d):
        rows = slice(8 * b, 8 * b + 8)
        east = p < NDIR // 2
        face, at = (UP, p) if east else (DOWN, p - NDIR // 2)
        centre = moved_ref[pl.ds(p * NFREQ + 8 * b, 8), :]
        one = one_ref[pl.ds(at * NFREQ + 8 * b, 8), :]
        two = two_ref[pl.ds(at * NFREQ + 8 * b, 8), :]
        row = jnp.where(even, one, two) if east else jnp.where(even, two, one)
        arrived = edge_ref[rows, p : p + 1]
        if SIN[d] >= 0:
            side, column = RIGHT, jnp.where(lane == LANES - 1, arrived, pltpu.roll(centre, LANES - 1, 1))
        else:
            side, column = LEFT, jnp.where(lane == 0, arrived, pltpu.roll(centre, 1, 1))
        value = (
            centre
            + abs(COS[d]) * (coef_ref[face, rows] * (row - centre))
            + abs(SIN[d]) * (coef_ref[side, rows] * (column - centre))
        )
        held_ref[pl.ds(p * NFREQ + 8 * b, 8), :] = value
        return value

    shared, stress = source_sums(propagated, spectrum_ref, coef_ref, spread_ref, vec_ref, step)

    values = jnp.concatenate(
        [
            cell_ref[CELLS * n : CELLS * n + CELLS, :] * jnp.concatenate([row] * 4, axis=1)
            for n, row in enumerate((stress, stress_ref[:1]))
        ],
        axis=0,
    )
    parts = []
    for _ in range(3):
        parts.append(values.astype(jnp.bfloat16))
        values = values - parts[-1].astype(jnp.float32)
    parts.append(jnp.zeros_like(parts[0]))
    cells = lax.dot_general(
        owner_ref[...], jnp.concatenate(parts, axis=0), (((1,), (1,)), ((), ())), preferred_element_type=jnp.float32
    )
    out_ref[pl.ds(LOCAL, NX, stride=SENT), :] = cells

    def adjoint_of(b, p, d):
        return held_ref[pl.ds(p * NFREQ + 8 * b, 8), :]

    def store(b, p, d, value):
        at = 8 * b * QUART * SENT + d // LOCAL * SENT + d % LOCAL
        out_ref[pl.ds(at, 8, stride=QUART * SENT), :] = value

    source_update(adjoint_of, store, coef_ref, spread_ref, shared, step)


def edges_kernel(arrived_ref, out_ref):
    lane = lane_iota(NX)
    quarter = lax.axis_index("comp") % QUART
    for north in (True, False):

        @pl.when((quarter < 2) == north)
        def _():
            edges = jnp.zeros((NX, LANES), jnp.float32)
            for j in range(LOCAL):
                value = arrived_ref[pl.ds(j, NX, stride=SENT), :]
                edges = jnp.where(lane == j, value[:, :1] if north else value[:, LANES - 1 :], edges)
            out_ref[:NX] = edges

    cells = arrived_ref[pl.ds(LOCAL, NX, stride=SENT), :]
    out_ref[NX:] = jnp.broadcast_to(jnp.sum(cells, axis=0, keepdims=True), (8, LANES))


def last_kernel(arrived_ref, mine_ref, edges_ref, face_ref, adjoint_ref, gradient_ref, held_ref, sems):
    tile = lax.axis_index("tile")
    quarter = lax.axis_index("comp") % QUART
    lane = lane_iota(NX)
    copies = [pltpu.make_async_copy(held_ref.at[j], adjoint_ref.at[j], sems.at[j]) for j in range(LOCAL)]
    for q in range(QUART):

        @pl.when(quarter == q)
        def _():
            for j in range(LOCAL):
                d = q * LOCAL + j
                centre = arrived_ref[pl.ds(j, NX, stride=SENT), :]
                arrived = edges_ref[:NX, j : j + 1]
                row = pltpu.roll(centre, NX - 1 if d in EAST else 1, 0)
                if SIN[q * LOCAL + 1] > 0:
                    column = jnp.where(lane == LANES - 1, arrived, pltpu.roll(centre, LANES - 1, 1))
                else:
                    column = jnp.where(lane == 0, arrived, pltpu.roll(centre, 1, 1))
                held_ref[j] = (
                    centre
                    + abs(COS[d]) * (face_ref[0] * (row - centre))
                    + abs(SIN[d]) * (face_ref[1] * (column - centre))
                )
                copies[j].start()

    cells = mine_ref[NX:] + edges_ref[NX:]
    cells = cells + pltpu.roll(cells, LANES - PART, 1) + pltpu.roll(cells, LANES - 2 * PART, 1)
    for n in range(NSTEP):
        at = pltpu.roll(cells, LANES - n * CELLS - tile * (CELLS // 2), 1)
        gradient_ref[n : n + 1, :] = at[:1, : CELLS // 2]
    for copy in copies:
        copy.wait()


def f32(*shape):
    return jax.ShapeDtypeStruct(shape, jnp.float32)


SPACES = {"s": pltpu.SMEM, "v": pltpu.VMEM, "h": pltpu.HBM}


def spec(spaces):
    return [pl.BlockSpec(memory_space=SPACES[space]) for space in spaces]


def call(kernel, inputs, outputs, out_shape, scratch=(), params=PARAMS):
    single = len(outputs) == 1
    return pl.pallas_call(
        kernel,
        in_specs=spec(inputs),
        out_specs=spec(outputs)[0] if single else tuple(spec(outputs)),
        out_shape=out_shape,
        scratch_shapes=list(scratch),
        compiler_params=params,
    )


def shards(
    adjoint_final,
    background,
    friction_velocity,
    wind_direction,
    refraction_rate,
    courant,
    growth_rate,
    dissipation_rate,
    sea_mask,
    interp_index,
    interp_weight,
):
    comp_count = lax.axis_size("comp")
    spectrum = background.reshape(NSTEP, NCOMP, LANES)
    held = [pltpu.VMEM((LOCAL, NX, LANES), jnp.float32), pltpu.SemaphoreType.DMA((LOCAL,))]
    sems = pltpu.SemaphoreType.DMA((CHUNKS,))
    by_row = call(
        by_row_kernel, "h", "h", f32(NCOMP, LANES), [held[0], sems, pltpu.VMEM((NCOMP, LANES), jnp.float32), sems], WHOLE
    )(adjoint_final)
    points = lax.all_to_all(by_row.reshape(NCOMP, 1, LANES), "comp", split_axis=0, concat_axis=0, tiled=True)
    points = points.reshape(NCOMP, LANES)
    coef, spread, vec, face, owner, cell = call(
        prepare_kernel,
        "vvvvsssvvv",
        "vvvvvv",
        (
            f32(13, NFREQ, LANES),
            f32(NSTEP, NDIR, LANES),
            f32(8, LANES),
            f32(2, NX, LANES),
            jax.ShapeDtypeStruct((NX, 4 * LANES), jnp.bfloat16),
            f32(PART, 4 * LANES),
        ),
    )(
        spectrum,
        friction_velocity.reshape(NSTEP, LANES),
        wind_direction.reshape(NSTEP, LANES),
        refraction_rate.reshape(NFREQ, LANES),
        courant,
        growth_rate,
        dissipation_rate,
        sea_mask,
        interp_index.reshape(4, LANES),
        interp_weight.reshape(4, LANES),
    )
    moved, one, two, edge, stress = call(
        first_source_kernel,
        "vvvvv",
        "vvvvv",
        (f32(NCOMP, LANES), f32(HALF, LANES), f32(HALF, LANES), f32(NFREQ, LANES), f32(8, LANES)),
    )(points, spectrum, coef, spread, vec)
    swap = [(0, 1), (1, 0)]
    last = comp_count - 1
    pairs = [(2 * i + t, 2 * (((i + 1) ^ 1) - 1) + t) for i in range(1, last) for t in range(2)]
    pairs += [(2 * i + t, 2 * i + 1 - t) for i in (0, last) for t in range(2)]
    one = lax.ppermute(one, "comp", [(i, i ^ 1) for i in range(comp_count)])
    two = lax.ppermute(two, ("comp", "tile"), pairs)
    edge = lax.ppermute(edge, "tile", swap)
    sent = call(
        second_source_kernel, "v" * 11, "v", f32(NX * SENT, LANES), [pltpu.VMEM((NCOMP, LANES), jnp.float32)]
    )(moved, one, two, edge, spectrum, coef, spread, vec, stress, owner, cell)
    arrived = lax.all_to_all(sent.reshape(NX * SENT, 1, LANES), "comp", split_axis=0, concat_axis=0, tiled=True)
    arrived = arrived.reshape(NX * SENT, LANES)
    mine = call(edges_kernel, "v", "v", f32(NX + 8, LANES))(arrived)
    theirs = lax.ppermute(mine, "tile", swap)
    adjoint, gradient = call(
        last_kernel, "vvvv", "hv", (f32(LOCAL, NX, LANES), f32(NSTEP, CELLS // 2)), held
    )(arrived, mine, theirs, face)
    return adjoint, gradient.T


def solution(mesh):
    in_specs = (
        P("comp", None, "tile"),
        P(None, None, "comp", "tile"),
        P(None, "comp", "tile"),
        P(None, "comp", "tile"),
        P(None, "comp", "tile"),
        P(),
        P(),
        P(),
        P(),
        P(None, "comp", "tile"),
        P(None, "comp", "tile"),
    )
    out_specs = (P("comp", None, "tile"), P(("comp", "tile"), None))
    return jax.shard_map(shards, mesh=mesh, in_specs=in_specs, out_specs=out_specs, check_vma=False)
```

```python
import math

import jax
import jax.numpy as jnp
import numpy as np
from jax import lax
from jax.experimental import pallas as pl
from jax.experimental.pallas import tpu as pltpu
from jax.sharding import PartitionSpec as P

NDIR = 36
NFREQ = 32
NSTEP = 2
NCOMP = NDIR * NFREQ
NX = 128
LANES = 128
LOCAL = 9
QUART = 4
SENT = LOCAL + 1
CHUNKS = 2
CELLS = 16

THETA = np.arange(NDIR) * (2.0 * math.pi / NDIR)
COS = [0.0 if d % 18 == 9 else math.cos(t) for d, t in enumerate(THETA)]
SIN = [0.0 if d % 18 == 0 else math.sin(t) for d, t in enumerate(THETA)]
EAST = list(range(27, NDIR)) + list(range(0, 9))
WEST = list(range(9, 27))
assert all(COS[d] >= 0 for d in EAST) and all(COS[d] <= 0 for d in WEST)
assert all(SIN[d] >= 0 for d in range(18)) and all(SIN[d] <= 0 for d in range(18, 36))
ORDER = EAST + WEST
PLACE = {d: p for p, d in enumerate(ORDER)}
HALF = len(EAST) * NFREQ

GROWTH, DISSIP, KEEP, TURN_NEG, TURN_POS, UP, DOWN, RIGHT, LEFT, GAIN0, GAIN1, LOSS0, LOSS1 = range(13)
GAIN, LOSS = (GAIN0, GAIN1), (LOSS0, LOSS1)
PART = NSTEP * CELLS

PARAMS = pltpu.CompilerParams(vmem_limit_bytes=24 * 1024 * 1024)
WHOLE = pltpu.CompilerParams(vmem_limit_bytes=60 * 1024 * 1024)


def lane_iota(rows):
    return lax.broadcasted_iota(jnp.int32, (rows, LANES), 1)


def sub_iota(rows):
    return lax.broadcasted_iota(jnp.int32, (rows, LANES), 0)


def by_row_kernel(in_ref, out_ref, held_ref, in_sems, rows_ref, out_sems):
    count = NX // CHUNKS
    ins, outs = [], []
    for c in range(CHUNKS):
        part = pl.ds(c * count, count)
        ins.append(pltpu.make_async_copy(in_ref.at[:, part, :], held_ref.at[:, part, :], in_sems.at[c]))
        part = pl.ds(c * count * LOCAL, count * LOCAL)
        outs.append(pltpu.make_async_copy(rows_ref.at[part, :], out_ref.at[part, :], out_sems.at[c]))
        ins[c].start()
    for c in range(CHUNKS):
        ins[c].wait()
        for j in range(LOCAL):
            rows_ref[pl.ds(c * count * LOCAL + j, count, stride=LOCAL), :] = held_ref[j, c * count : (c + 1) * count]
        outs[c].start()
    for copy in outs:
        copy.wait()


def prepare_kernel(
    spectrum_ref, friction_ref, wind_ref, refraction_ref, courant_ref, growth_ref, dissip_ref, mask_ref,
    index_ref, weight_ref, coef_ref, spread_ref, vec_ref, face_ref, owner_ref, cell_ref,
):
    row = lax.axis_index("comp")
    tile = lax.axis_index("tile")
    left_half = mask_ref[:, :LANES].astype(jnp.float32)
    right_half = mask_ref[:, LANES:].astype(jnp.float32)
    first = tile == 0
    own = jnp.where(first, left_half, right_half)
    lane = lane_iota(NX)
    sub = sub_iota(NX)
    other = jnp.where(first, right_half, left_half)
    nxt = jnp.where(lane == LANES - 1, jnp.where(first, pltpu.roll(other, LANES - 1, 1), 0.0), pltpu.roll(own, LANES - 1, 1))
    prv = jnp.where(lane == 0, jnp.where(first, 0.0, pltpu.roll(other, 1, 1)), pltpu.roll(own, 1, 1))
    quarter = row % QUART
    speed = courant_ref[row // QUART]
    up = own * jnp.where(sub == NX - 1, 0.0, pltpu.roll(own, NX - 1, 0))
    down = own * jnp.where(sub == 0, 0.0, pltpu.roll(own, 1, 0))
    right, left = own * nxt, own * prv
    face_ref[0] = speed * jnp.where((quarter == 0) | (quarter == 3), up, down)
    face_ref[1] = speed * jnp.where(quarter < 2, right, left)
    pick = sub == row
    mask, *faces = [
        jnp.sum(jnp.where(pick, value, 0.0), axis=0, keepdims=True) for value in (own, up, down, right, left)
    ]

    sub_f = sub_iota(NFREQ)
    growth = jnp.zeros((NFREQ, LANES), jnp.float32)
    dissip = jnp.zeros((NFREQ, LANES), jnp.float32)
    courant = jnp.zeros((NFREQ, LANES), jnp.float32)
    for f in range(NFREQ):
        at = sub_f == f
        growth = jnp.where(at, growth_ref[f], growth)
        dissip = jnp.where(at, dissip_ref[f], dissip)
        courant = jnp.where(at, courant_ref[f], courant)
    turn = refraction_ref[...]
    coef_ref[GROWTH] = growth
    coef_ref[DISSIP] = dissip
    coef_ref[KEEP] = 1.0 - jnp.abs(turn)
    coef_ref[TURN_NEG] = jnp.minimum(turn, 0.0)
    coef_ref[TURN_POS] = jnp.maximum(turn, 0.0)
    for k, name in enumerate((UP, DOWN, RIGHT, LEFT)):
        coef_ref[name] = courant * faces[k]
    vec_ref[...] = jnp.zeros_like(vec_ref)
    vec_ref[2:3] = mask
    theta = sub_iota(NDIR).astype(jnp.float32) * (2.0 * math.pi / NDIR)
    for n in range(NSTEP):
        total = jnp.zeros((8, LANES), jnp.float32)
        for k in range(NCOMP // 8):
            total = total + spectrum_ref[n, pl.ds(8 * k, 8), :]
        energy = jnp.sum(total, axis=0, keepdims=True) / NFREQ
        vec_ref[n : n + 1] = (2.0 / NFREQ) * energy * mask
        coef_ref[GAIN[n]] = growth * (friction_ref[n : n + 1] * mask)
        coef_ref[LOSS[n]] = mask - dissip * (energy * energy * mask)
        spread_ref[n] = jnp.maximum(jnp.cos(theta - wind_ref[n : n + 1]), 0.0)

    sub_c = sub_iota(PART)
    for corner in range(4):
        lanes = slice(corner * LANES, (corner + 1) * LANES)
        index = index_ref[corner : corner + 1, :]
        owner_ref[:, lanes] = jnp.where(sub == index // CELLS, 1.0, 0.0).astype(jnp.bfloat16)
        cell_ref[:, lanes] = jnp.where(sub_c % CELLS == index % CELLS, weight_ref[corner : corner + 1, :], 0.0)


def source_sums(adjoint_of, spectrum_ref, coef_ref, spread_ref, vec_ref, step):
    damped = jnp.zeros((8, LANES), jnp.float32)
    stress = jnp.zeros((8, LANES), jnp.float32)
    for b in range(NFREQ // 8):
        plain = jnp.zeros((8, LANES), jnp.float32)
        spread = jnp.zeros((8, LANES), jnp.float32)
        for p, d in enumerate(ORDER):
            product = spectrum_ref[step, pl.ds(8 * b * NDIR + d, 8, stride=NDIR), :] * adjoint_of(b, p, d)
            plain = plain + product
            spread = spread + spread_ref[step, d : d + 1, :] * product
        damped = damped + coef_ref[DISSIP, 8 * b : 8 * b + 8] * plain
        stress = stress + coef_ref[GROWTH, 8 * b : 8 * b + 8] * spread
    damped = jnp.sum(damped, axis=0, keepdims=True)
    stress = jnp.sum(stress, axis=0, keepdims=True)
    return vec_ref[step : step + 1] * damped, vec_ref[2:3] * stress


def source_update(adjoint_of, store, coef_ref, spread_ref, shared, step):
    shared = jnp.broadcast_to(shared, (8, LANES))
    for b in range(NFREQ // 8):
        rows = slice(8 * b, 8 * b + 8)
        gain, loss = coef_ref[GAIN[step], rows], coef_ref[LOSS[step], rows]
        keep, neg, pos = coef_ref[KEEP, rows], coef_ref[TURN_NEG, rows], coef_ref[TURN_POS, rows]

        def updated(d):
            return adjoint_of(b, PLACE[d], d) * (loss + gain * spread_ref[step, d : d + 1, :]) - shared

        before, here, first = updated(ORDER[-1]), updated(ORDER[0]), None
        first = here
        for p, d in enumerate(ORDER):
            after = updated(ORDER[p + 1]) if p + 1 < NDIR else first
            store(b, p, d, keep * here - neg * before + pos * after)
            before, here = here, after


def first_source_kernel(
    adjoint_ref, spectrum_ref, coef_ref, spread_ref, vec_ref, moved_ref, one_ref, two_ref, edge_ref, stress_ref
):
    step = NSTEP - 1

    def adjoint_of(b, p, d):
        return adjoint_ref[pl.ds(8 * b * NDIR + d, 8, stride=NDIR), :]

    shared, stress = source_sums(adjoint_of, spectrum_ref, coef_ref, spread_ref, vec_ref, step)
    stress_ref[...] = jnp.broadcast_to(stress, (8, LANES))
    lane = lane_iota(8)
    edges = [jnp.zeros((8, LANES), jnp.float32) for _ in range(NFREQ // 8)]

    def store(b, p, d, value):
        moved_ref[pl.ds(p * NFREQ + 8 * b, 8), :] = value
        column = value[:, :1] if SIN[d] >= 0 else value[:, LANES - 1 :]
        edges[b] = jnp.where(lane == p, column, edges[b])

    source_update(adjoint_of, store, coef_ref, spread_ref, shared, step)
    for b in range(NFREQ // 8):
        edge_ref[8 * b : 8 * b + 8] = edges[b]
    odd = lax.axis_index("comp") % 2

    @pl.when(odd == 1)
    def _():
        one_ref[...] = moved_ref[:HALF]
        two_ref[...] = moved_ref[HALF:]

    @pl.when(odd == 0)
    def _():
        one_ref[...] = moved_ref[HALF:]
        two_ref[...] = moved_ref[:HALF]


def propagate_half(east, moved_ref, near_ref, edge_ref, spectrum_ref, coef_ref, spread_ref, half_ref, sums_ref):
    step = 0
    lane = lane_iota(8)
    half = NDIR // 2
    face, start = (UP, 0) if east else (DOWN, half)
    damped = jnp.zeros((8, LANES), jnp.float32)
    stress = jnp.zeros((8, LANES), jnp.float32)
    for b in range(NFREQ // 8):
        rows = slice(8 * b, 8 * b + 8)
        plain = jnp.zeros((8, LANES), jnp.float32)
        spread = jnp.zeros((8, LANES), jnp.float32)
        for at in range(half):
            p = start + at
            d = ORDER[p]
            centre = moved_ref[pl.ds(p * NFREQ + 8 * b, 8), :]
            row = near_ref[pl.ds(at * NFREQ + 8 * b, 8), :]
            arrived = edge_ref[rows, p : p + 1]
            if SIN[d] >= 0:
                side, column = RIGHT, jnp.where(lane == LANES - 1, arrived, pltpu.roll(centre, LANES - 1, 1))
            else:
                side, column = LEFT, jnp.where(lane == 0, arrived, pltpu.roll(centre, 1, 1))
            value = (
                centre
                + abs(COS[d]) * (coef_ref[face, rows] * (row - centre))
                + abs(SIN[d]) * (coef_ref[side, rows] * (column - centre))
            )
            half_ref[pl.ds(at * NFREQ + 8 * b, 8), :] = value
            product = spectrum_ref[step, pl.ds(8 * b * NDIR + d, 8, stride=NDIR), :] * value
            plain = plain + product
            spread = spread + spread_ref[step, d : d + 1, :] * product
        damped = damped + coef_ref[DISSIP, rows] * plain
        stress = stress + coef_ref[GROWTH, rows] * spread
    sums_ref[:8] = damped
    sums_ref[8:] = stress


def first_half_kernel(moved_ref, one_ref, edge_ref, spectrum_ref, coef_ref, spread_ref, half_ref, sums_ref):
    odd = lax.axis_index("comp") % 2
    for parity, east in ((0, True), (1, False)):

        @pl.when(odd == parity)
        def _():
            propagate_half(east, moved_ref, one_ref, edge_ref, spectrum_ref, coef_ref, spread_ref, half_ref, sums_ref)


def second_source_kernel(
    moved_ref, two_ref, edge_ref, spectrum_ref, coef_ref, spread_ref, vec_ref, stress_ref,
    owner_ref, cell_ref, done_ref, done_sums_ref, out_ref, half_ref, sums_ref,
):
    step = 0
    odd = lax.axis_index("comp") % 2
    even = jnp.broadcast_to(odd, (8, LANES)) == 0
    for parity, east in ((0, False), (1, True)):

        @pl.when(odd == parity)
        def _():
            propagate_half(east, moved_ref, two_ref, edge_ref, spectrum_ref, coef_ref, spread_ref, half_ref, sums_ref)

    damped = jnp.sum(done_sums_ref[:8] + sums_ref[:8], axis=0, keepdims=True)
    stress = jnp.sum(done_sums_ref[8:] + sums_ref[8:], axis=0, keepdims=True)
    shared, stress = vec_ref[step : step + 1] * damped, vec_ref[2:3] * stress

    values = jnp.concatenate(
        [
            cell_ref[CELLS * n : CELLS * n + CELLS, :] * jnp.concatenate([row] * 4, axis=1)
            for n, row in enumerate((stress, stress_ref[:1]))
        ],
        axis=0,
    )
    parts = []
    for _ in range(3):
        parts.append(values.astype(jnp.bfloat16))
        values = values - parts[-1].astype(jnp.float32)
    parts.append(jnp.zeros_like(parts[0]))
    cells = lax.dot_general(
        owner_ref[...], jnp.concatenate(parts, axis=0), (((1,), (1,)), ((), ())), preferred_element_type=jnp.float32
    )
    out_ref[pl.ds(LOCAL, NX, stride=SENT), :] = cells

    def adjoint_of(b, p, d):
        east = p < NDIR // 2
        rows = pl.ds((p if east else p - NDIR // 2) * NFREQ + 8 * b, 8)
        done, here = done_ref[rows, :], half_ref[rows, :]
        return jnp.where(even, done, here) if east else jnp.where(even, here, done)

    def store(b, p, d, value):
        at = 8 * b * QUART * SENT + d // LOCAL * SENT + d % LOCAL
        out_ref[pl.ds(at, 8, stride=QUART * SENT), :] = value

    source_update(adjoint_of, store, coef_ref, spread_ref, shared, step)


def edges_kernel(arrived_ref, out_ref):
    lane = lane_iota(NX)
    quarter = lax.axis_index("comp") % QUART
    for north in (True, False):

        @pl.when((quarter < 2) == north)
        def _():
            edges = jnp.zeros((NX, LANES), jnp.float32)
            for j in range(LOCAL):
                value = arrived_ref[pl.ds(j, NX, stride=SENT), :]
                edges = jnp.where(lane == j, value[:, :1] if north else value[:, LANES - 1 :], edges)
            out_ref[:NX] = edges

    cells = arrived_ref[pl.ds(LOCAL, NX, stride=SENT), :]
    out_ref[NX:] = jnp.broadcast_to(jnp.sum(cells, axis=0, keepdims=True), (8, LANES))


def last_kernel(arrived_ref, mine_ref, edges_ref, face_ref, adjoint_ref, gradient_ref, held_ref, sems):
    tile = lax.axis_index("tile")
    quarter = lax.axis_index("comp") % QUART
    lane = lane_iota(NX)
    copies = [pltpu.make_async_copy(held_ref.at[j], adjoint_ref.at[j], sems.at[j]) for j in range(LOCAL)]
    for q in range(QUART):

        @pl.when(quarter == q)
        def _():
            for j in range(LOCAL):
                d = q * LOCAL + j
                centre = arrived_ref[pl.ds(j, NX, stride=SENT), :]
                arrived = edges_ref[:NX, j : j + 1]
                row = pltpu.roll(centre, NX - 1 if d in EAST else 1, 0)
                if SIN[q * LOCAL + 1] > 0:
                    column = jnp.where(lane == LANES - 1, arrived, pltpu.roll(centre, LANES - 1, 1))
                else:
                    column = jnp.where(lane == 0, arrived, pltpu.roll(centre, 1, 1))
                held_ref[j] = (
                    centre
                    + abs(COS[d]) * (face_ref[0] * (row - centre))
                    + abs(SIN[d]) * (face_ref[1] * (column - centre))
                )
                copies[j].start()

    cells = mine_ref[NX:] + edges_ref[NX:]
    cells = cells + pltpu.roll(cells, LANES - PART, 1) + pltpu.roll(cells, LANES - 2 * PART, 1)
    for n in range(NSTEP):
        at = pltpu.roll(cells, LANES - n * CELLS - tile * (CELLS // 2), 1)
        gradient_ref[n : n + 1, :] = at[:1, : CELLS // 2]
    for copy in copies:
        copy.wait()


def f32(*shape):
    return jax.ShapeDtypeStruct(shape, jnp.float32)


SPACES = {"s": pltpu.SMEM, "v": pltpu.VMEM, "h": pltpu.HBM}


def spec(spaces):
    return [pl.BlockSpec(memory_space=SPACES[space]) for space in spaces]


def call(kernel, inputs, outputs, out_shape, scratch=(), params=PARAMS):
    single = len(outputs) == 1
    return pl.pallas_call(
        kernel,
        in_specs=spec(inputs),
        out_specs=spec(outputs)[0] if single else tuple(spec(outputs)),
        out_shape=out_shape,
        scratch_shapes=list(scratch),
        compiler_params=params,
    )


def shards(
    adjoint_final,
    background,
    friction_velocity,
    wind_direction,
    refraction_rate,
    courant,
    growth_rate,
    dissipation_rate,
    sea_mask,
    interp_index,
    interp_weight,
):
    comp_count = lax.axis_size("comp")
    spectrum = background.reshape(NSTEP, NCOMP, LANES)
    held = [pltpu.VMEM((LOCAL, NX, LANES), jnp.float32), pltpu.SemaphoreType.DMA((LOCAL,))]
    sems = pltpu.SemaphoreType.DMA((CHUNKS,))
    by_row = call(
        by_row_kernel, "h", "h", f32(NCOMP, LANES), [held[0], sems, pltpu.VMEM((NCOMP, LANES), jnp.float32), sems], WHOLE
    )(adjoint_final)
    points = lax.all_to_all(by_row.reshape(NCOMP, 1, LANES), "comp", split_axis=0, concat_axis=0, tiled=True)
    points = points.reshape(NCOMP, LANES)
    coef, spread, vec, face, owner, cell = call(
        prepare_kernel,
        "vvvvsssvvv",
        "vvvvvv",
        (
            f32(13, NFREQ, LANES),
            f32(NSTEP, NDIR, LANES),
            f32(8, LANES),
            f32(2, NX, LANES),
            jax.ShapeDtypeStruct((NX, 4 * LANES), jnp.bfloat16),
            f32(PART, 4 * LANES),
        ),
    )(
        spectrum,
        friction_velocity.reshape(NSTEP, LANES),
        wind_direction.reshape(NSTEP, LANES),
        refraction_rate.reshape(NFREQ, LANES),
        courant,
        growth_rate,
        dissipation_rate,
        sea_mask,
        interp_index.reshape(4, LANES),
        interp_weight.reshape(4, LANES),
    )
    moved, one, two, edge, stress = call(
        first_source_kernel,
        "vvvvv",
        "vvvvv",
        (f32(NCOMP, LANES), f32(HALF, LANES), f32(HALF, LANES), f32(NFREQ, LANES), f32(8, LANES)),
    )(points, spectrum, coef, spread, vec)
    swap = [(0, 1), (1, 0)]
    last = comp_count - 1
    pairs = [(2 * i + t, 2 * (((i + 1) ^ 1) - 1) + t) for i in range(1, last) for t in range(2)]
    pairs += [(2 * i + t, 2 * i + 1 - t) for i in (0, last) for t in range(2)]
    one = lax.ppermute(one, "comp", [(i, i ^ 1) for i in range(comp_count)])
    two = lax.ppermute(two, ("comp", "tile"), pairs)
    edge = lax.ppermute(edge, "tile", swap)
    done, done_sums = call(first_half_kernel, "v" * 6, "vv", (f32(HALF, LANES), f32(16, LANES)))(
        moved, one, edge, spectrum, coef, spread
    )
    sent = call(
        second_source_kernel,
        "v" * 12,
        "v",
        f32(NX * SENT, LANES),
        [pltpu.VMEM((HALF, LANES), jnp.float32), pltpu.VMEM((16, LANES), jnp.float32)],
    )(moved, two, edge, spectrum, coef, spread, vec, stress, owner, cell, done, done_sums)
    arrived = lax.all_to_all(sent.reshape(NX * SENT, 1, LANES), "comp", split_axis=0, concat_axis=0, tiled=True)
    arrived = arrived.reshape(NX * SENT, LANES)
    mine = call(edges_kernel, "v", "v", f32(NX + 8, LANES))(arrived)
    theirs = lax.ppermute(mine, "tile", swap)
    adjoint, gradient = call(
        last_kernel, "vvvv", "hv", (f32(LOCAL, NX, LANES), f32(NSTEP, CELLS // 2)), held
    )(arrived, mine, theirs, face)
    return adjoint, gradient.T


def solution(mesh):
    in_specs = (
        P("comp", None, "tile"),
        P(None, None, "comp", "tile"),
        P(None, "comp", "tile"),
        P(None, "comp", "tile"),
        P(None, "comp", "tile"),
        P(),
        P(),
        P(),
        P(),
        P(None, "comp", "tile"),
        P(None, "comp", "tile"),
    )
    out_specs = (P("comp", None, "tile"), P(("comp", "tile"), None))
    return jax.shard_map(shards, mesh=mesh, in_specs=in_specs, out_specs=out_specs, check_vma=False)
```

```python
import math

import jax
import jax.numpy as jnp
import numpy as np
from jax import lax
from jax.experimental import pallas as pl
from jax.experimental.pallas import tpu as pltpu
from jax.sharding import PartitionSpec as P

NDIR = 36
NFREQ = 32
NSTEP = 2
NCOMP = NDIR * NFREQ
NX = 128
LANES = 128
LOCAL = 9
QUART = 4
SENT = LOCAL + 1
CHUNKS = 2
CELLS = 16

THETA = np.arange(NDIR) * (2.0 * math.pi / NDIR)
COS = [0.0 if d % 18 == 9 else math.cos(t) for d, t in enumerate(THETA)]
SIN = [0.0 if d % 18 == 0 else math.sin(t) for d, t in enumerate(THETA)]
EAST = list(range(27, NDIR)) + list(range(0, 9))
WEST = list(range(9, 27))
assert all(COS[d] >= 0 for d in EAST) and all(COS[d] <= 0 for d in WEST)
assert all(SIN[d] >= 0 for d in range(18)) and all(SIN[d] <= 0 for d in range(18, 36))
ORDER = EAST + WEST
PLACE = {d: p for p, d in enumerate(ORDER)}
HALF = len(EAST) * NFREQ

GROWTH, DISSIP, KEEP, TURN_NEG, TURN_POS, UP, DOWN, RIGHT, LEFT, GAIN0, GAIN1, LOSS0, LOSS1 = range(13)
GAIN, LOSS = (GAIN0, GAIN1), (LOSS0, LOSS1)
PART = NSTEP * CELLS

PARAMS = pltpu.CompilerParams(vmem_limit_bytes=24 * 1024 * 1024)
WHOLE = pltpu.CompilerParams(vmem_limit_bytes=60 * 1024 * 1024)


def lane_iota(rows):
    return lax.broadcasted_iota(jnp.int32, (rows, LANES), 1)


def sub_iota(rows):
    return lax.broadcasted_iota(jnp.int32, (rows, LANES), 0)


def by_row_kernel(in_ref, out_ref, held_ref, in_sems, rows_ref, out_sems):
    count = NX // CHUNKS
    ins, outs = [], []
    for c in range(CHUNKS):
        part = pl.ds(c * count, count)
        ins.append(pltpu.make_async_copy(in_ref.at[:, part, :], held_ref.at[:, part, :], in_sems.at[c]))
        part = pl.ds(c * count * LOCAL, count * LOCAL)
        outs.append(pltpu.make_async_copy(rows_ref.at[part, :], out_ref.at[part, :], out_sems.at[c]))
        ins[c].start()
    for c in range(CHUNKS):
        ins[c].wait()
        for j in range(LOCAL):
            rows_ref[pl.ds(c * count * LOCAL + j, count, stride=LOCAL), :] = held_ref[j, c * count : (c + 1) * count]
        outs[c].start()
    for copy in outs:
        copy.wait()


def prepare_kernel(
    spectrum_ref, friction_ref, wind_ref, refraction_ref, courant_ref, growth_ref, dissip_ref, mask_ref,
    index_ref, weight_ref, coef_ref, spread_ref, vec_ref, face_ref, owner_ref, cell_ref,
):
    row = lax.axis_index("comp")
    tile = lax.axis_index("tile")
    left_half = mask_ref[:, :LANES].astype(jnp.float32)
    right_half = mask_ref[:, LANES:].astype(jnp.float32)
    first = tile == 0
    own = jnp.where(first, left_half, right_half)
    lane = lane_iota(NX)
    sub = sub_iota(NX)
    other = jnp.where(first, right_half, left_half)
    nxt = jnp.where(lane == LANES - 1, jnp.where(first, pltpu.roll(other, LANES - 1, 1), 0.0), pltpu.roll(own, LANES - 1, 1))
    prv = jnp.where(lane == 0, jnp.where(first, 0.0, pltpu.roll(other, 1, 1)), pltpu.roll(own, 1, 1))
    quarter = row % QUART
    speed = courant_ref[row // QUART]
    up = own * jnp.where(sub == NX - 1, 0.0, pltpu.roll(own, NX - 1, 0))
    down = own * jnp.where(sub == 0, 0.0, pltpu.roll(own, 1, 0))
    right, left = own * nxt, own * prv
    face_ref[0] = speed * jnp.where((quarter == 0) | (quarter == 3), up, down)
    face_ref[1] = speed * jnp.where(quarter < 2, right, left)
    pick = sub == row
    mask, *faces = [
        jnp.sum(jnp.where(pick, value, 0.0), axis=0, keepdims=True) for value in (own, up, down, right, left)
    ]

    sub_f = sub_iota(NFREQ)
    growth = jnp.zeros((NFREQ, LANES), jnp.float32)
    dissip = jnp.zeros((NFREQ, LANES), jnp.float32)
    courant = jnp.zeros((NFREQ, LANES), jnp.float32)
    for f in range(NFREQ):
        at = sub_f == f
        growth = jnp.where(at, growth_ref[f], growth)
        dissip = jnp.where(at, dissip_ref[f], dissip)
        courant = jnp.where(at, courant_ref[f], courant)
    turn = refraction_ref[...]
    coef_ref[GROWTH] = growth
    coef_ref[DISSIP] = dissip
    coef_ref[KEEP] = 1.0 - jnp.abs(turn)
    coef_ref[TURN_NEG] = jnp.minimum(turn, 0.0)
    coef_ref[TURN_POS] = jnp.maximum(turn, 0.0)
    for k, name in enumerate((UP, DOWN, RIGHT, LEFT)):
        coef_ref[name] = courant * faces[k]
    vec_ref[...] = jnp.zeros_like(vec_ref)
    vec_ref[2:3] = mask
    theta = sub_iota(NDIR).astype(jnp.float32) * (2.0 * math.pi / NDIR)
    for n in range(NSTEP):
        total = jnp.zeros((8, LANES), jnp.float32)
        for k in range(NCOMP // 8):
            total = total + spectrum_ref[n, pl.ds(8 * k, 8), :]
        energy = jnp.sum(total, axis=0, keepdims=True) / NFREQ
        vec_ref[n : n + 1] = (2.0 / NFREQ) * energy * mask
        coef_ref[GAIN[n]] = growth * (friction_ref[n : n + 1] * mask)
        coef_ref[LOSS[n]] = mask - dissip * (energy * energy * mask)
        spread_ref[n] = jnp.maximum(jnp.cos(theta - wind_ref[n : n + 1]), 0.0)

    sub_c = sub_iota(PART)
    for corner in range(4):
        lanes = slice(corner * LANES, (corner + 1) * LANES)
        index = index_ref[corner : corner + 1, :]
        owner_ref[:, lanes] = jnp.where(sub == index // CELLS, 1.0, 0.0).astype(jnp.bfloat16)
        cell_ref[:, lanes] = jnp.where(sub_c % CELLS == index % CELLS, weight_ref[corner : corner + 1, :], 0.0)


def source_sums(adjoint_of, spectrum_ref, coef_ref, spread_ref, vec_ref, step):
    damped = jnp.zeros((8, LANES), jnp.float32)
    stress = jnp.zeros((8, LANES), jnp.float32)
    for b in range(NFREQ // 8):
        plain = jnp.zeros((8, LANES), jnp.float32)
        spread = jnp.zeros((8, LANES), jnp.float32)
        for p, d in enumerate(ORDER):
            product = spectrum_ref[step, pl.ds(8 * b * NDIR + d, 8, stride=NDIR), :] * adjoint_of(b, p, d)
            plain = plain + product
            spread = spread + spread_ref[step, d : d + 1, :] * product
        damped = damped + coef_ref[DISSIP, 8 * b : 8 * b + 8] * plain
        stress = stress + coef_ref[GROWTH, 8 * b : 8 * b + 8] * spread
    damped = jnp.sum(damped, axis=0, keepdims=True)
    stress = jnp.sum(stress, axis=0, keepdims=True)
    return vec_ref[step : step + 1] * damped, vec_ref[2:3] * stress


def source_update(adjoint_of, store, coef_ref, spread_ref, shared, step):
    shared = jnp.broadcast_to(shared, (8, LANES))
    for b in range(NFREQ // 8):
        rows = slice(8 * b, 8 * b + 8)
        gain, loss = coef_ref[GAIN[step], rows], coef_ref[LOSS[step], rows]
        keep, neg, pos = coef_ref[KEEP, rows], coef_ref[TURN_NEG, rows], coef_ref[TURN_POS, rows]

        def updated(d):
            return adjoint_of(b, PLACE[d], d) * (loss + gain * spread_ref[step, d : d + 1, :]) - shared

        before, here, first = updated(ORDER[-1]), updated(ORDER[0]), None
        first = here
        for p, d in enumerate(ORDER):
            after = updated(ORDER[p + 1]) if p + 1 < NDIR else first
            store(b, p, d, keep * here - neg * before + pos * after)
            before, here = here, after


def first_source_kernel(
    adjoint_ref, spectrum_ref, coef_ref, spread_ref, vec_ref, moved_ref, one_ref, two_ref, edge_ref, stress_ref
):
    step = NSTEP - 1

    def adjoint_of(b, p, d):
        return adjoint_ref[pl.ds(8 * b * NDIR + d, 8, stride=NDIR), :]

    shared, stress = source_sums(adjoint_of, spectrum_ref, coef_ref, spread_ref, vec_ref, step)
    stress_ref[...] = jnp.broadcast_to(stress, (8, LANES))
    lane = lane_iota(8)
    half = NDIR // 2
    odd = lax.axis_index("comp") % 2
    for parity in range(2):

        @pl.when(odd == parity)
        def _():
            edges = [jnp.zeros((8, LANES), jnp.float32) for _ in range(NFREQ // 8)]

            def store(b, p, d, value):
                moved_ref[pl.ds(p * NFREQ + 8 * b, 8), :] = value
                sent_ref = one_ref if (p < half) == (parity == 1) else two_ref
                sent_ref[pl.ds(p % half * NFREQ + 8 * b, 8), :] = value
                column = value[:, :1] if SIN[d] >= 0 else value[:, LANES - 1 :]
                edges[b] = jnp.where(lane == p, column, edges[b])

            source_update(adjoint_of, store, coef_ref, spread_ref, shared, step)
            for b in range(NFREQ // 8):
                edge_ref[8 * b : 8 * b + 8] = edges[b]


def propagate_half(east, moved_ref, near_ref, edge_ref, spectrum_ref, coef_ref, spread_ref, half_ref, sums_ref):
    step = 0
    lane = lane_iota(8)
    half = NDIR // 2
    face, start = (UP, 0) if east else (DOWN, half)
    damped = jnp.zeros((8, LANES), jnp.float32)
    stress = jnp.zeros((8, LANES), jnp.float32)
    for b in range(NFREQ // 8):
        rows = slice(8 * b, 8 * b + 8)
        plain = jnp.zeros((8, LANES), jnp.float32)
        spread = jnp.zeros((8, LANES), jnp.float32)
        for at in range(half):
            p = start + at
            d = ORDER[p]
            centre = moved_ref[pl.ds(p * NFREQ + 8 * b, 8), :]
            row = near_ref[pl.ds(at * NFREQ + 8 * b, 8), :]
            arrived = edge_ref[rows, p : p + 1]
            if SIN[d] >= 0:
                side, column = RIGHT, jnp.where(lane == LANES - 1, arrived, pltpu.roll(centre, LANES - 1, 1))
            else:
                side, column = LEFT, jnp.where(lane == 0, arrived, pltpu.roll(centre, 1, 1))
            value = (
                centre
                + abs(COS[d]) * (coef_ref[face, rows] * (row - centre))
                + abs(SIN[d]) * (coef_ref[side, rows] * (column - centre))
            )
            half_ref[pl.ds(at * NFREQ + 8 * b, 8), :] = value
            product = spectrum_ref[step, pl.ds(8 * b * NDIR + d, 8, stride=NDIR), :] * value
            plain = plain + product
            spread = spread + spread_ref[step, d : d + 1, :] * product
        damped = damped + coef_ref[DISSIP, rows] * plain
        stress = stress + coef_ref[GROWTH, rows] * spread
    sums_ref[:8] = damped
    sums_ref[8:] = stress


def first_half_kernel(moved_ref, one_ref, edge_ref, spectrum_ref, coef_ref, spread_ref, half_ref, sums_ref):
    odd = lax.axis_index("comp") % 2
    for parity, east in ((0, True), (1, False)):

        @pl.when(odd == parity)
        def _():
            propagate_half(east, moved_ref, one_ref, edge_ref, spectrum_ref, coef_ref, spread_ref, half_ref, sums_ref)


def second_source_kernel(
    moved_ref, two_ref, edge_ref, spectrum_ref, coef_ref, spread_ref, vec_ref, stress_ref,
    owner_ref, cell_ref, done_ref, done_sums_ref, out_ref, half_ref, sums_ref,
):
    step = 0
    odd = lax.axis_index("comp") % 2
    for parity, east in ((0, False), (1, True)):

        @pl.when(odd == parity)
        def _():
            propagate_half(east, moved_ref, two_ref, edge_ref, spectrum_ref, coef_ref, spread_ref, half_ref, sums_ref)

    damped = jnp.sum(done_sums_ref[:8] + sums_ref[:8], axis=0, keepdims=True)
    stress = jnp.sum(done_sums_ref[8:] + sums_ref[8:], axis=0, keepdims=True)
    shared, stress = vec_ref[step : step + 1] * damped, vec_ref[2:3] * stress

    values = jnp.concatenate(
        [
            cell_ref[CELLS * n : CELLS * n + CELLS, :] * jnp.concatenate([row] * 4, axis=1)
            for n, row in enumerate((stress, stress_ref[:1]))
        ],
        axis=0,
    )
    parts = []
    for _ in range(3):
        parts.append(values.astype(jnp.bfloat16))
        values = values - parts[-1].astype(jnp.float32)
    parts.append(jnp.zeros_like(parts[0]))
    cells = lax.dot_general(
        owner_ref[...], jnp.concatenate(parts, axis=0), (((1,), (1,)), ((), ())), preferred_element_type=jnp.float32
    )
    out_ref[pl.ds(LOCAL, NX, stride=SENT), :] = cells

    def store(b, p, d, value):
        at = 8 * b * QUART * SENT + d // LOCAL * SENT + d % LOCAL
        out_ref[pl.ds(at, 8, stride=QUART * SENT), :] = value

    for parity in range(2):

        @pl.when(odd == parity)
        def _():
            def adjoint_of(b, p, d):
                ref = done_ref if (p < NDIR // 2) == (parity == 0) else half_ref
                return ref[pl.ds(p % (NDIR // 2) * NFREQ + 8 * b, 8), :]

            source_update(adjoint_of, store, coef_ref, spread_ref, shared, step)


def edges_kernel(arrived_ref, out_ref):
    lane = lane_iota(NX)
    quarter = lax.axis_index("comp") % QUART
    for north in (True, False):

        @pl.when((quarter < 2) == north)
        def _():
            edges = jnp.zeros((NX, LANES), jnp.float32)
            for j in range(LOCAL):
                value = arrived_ref[pl.ds(j, NX, stride=SENT), :]
                edges = jnp.where(lane == j, value[:, :1] if north else value[:, LANES - 1 :], edges)
            out_ref[:NX] = edges

    cells = arrived_ref[pl.ds(LOCAL, NX, stride=SENT), :]
    out_ref[NX:] = jnp.broadcast_to(jnp.sum(cells, axis=0, keepdims=True), (8, LANES))


def last_kernel(arrived_ref, mine_ref, edges_ref, face_ref, adjoint_ref, gradient_ref, held_ref, sems):
    tile = lax.axis_index("tile")
    quarter = lax.axis_index("comp") % QUART
    lane = lane_iota(NX)
    copies = [pltpu.make_async_copy(held_ref.at[j], adjoint_ref.at[j], sems.at[j]) for j in range(LOCAL)]
    for q in range(QUART):

        @pl.when(quarter == q)
        def _():
            for j in range(LOCAL):
                d = q * LOCAL + j
                centre = arrived_ref[pl.ds(j, NX, stride=SENT), :]
                arrived = edges_ref[:NX, j : j + 1]
                row = pltpu.roll(centre, NX - 1 if d in EAST else 1, 0)
                if SIN[q * LOCAL + 1] > 0:
                    column = jnp.where(lane == LANES - 1, arrived, pltpu.roll(centre, LANES - 1, 1))
                else:
                    column = jnp.where(lane == 0, arrived, pltpu.roll(centre, 1, 1))
                held_ref[j] = (
                    centre
                    + abs(COS[d]) * (face_ref[0] * (row - centre))
                    + abs(SIN[d]) * (face_ref[1] * (column - centre))
                )
                copies[j].start()

    cells = mine_ref[NX:] + edges_ref[NX:]
    cells = cells + pltpu.roll(cells, LANES - PART, 1) + pltpu.roll(cells, LANES - 2 * PART, 1)
    for n in range(NSTEP):
        at = pltpu.roll(cells, LANES - n * CELLS - tile * (CELLS // 2), 1)
        gradient_ref[n : n + 1, :] = at[:1, : CELLS // 2]
    for copy in copies:
        copy.wait()


def f32(*shape):
    return jax.ShapeDtypeStruct(shape, jnp.float32)


SPACES = {"s": pltpu.SMEM, "v": pltpu.VMEM, "h": pltpu.HBM}


def spec(spaces):
    return [pl.BlockSpec(memory_space=SPACES[space]) for space in spaces]


def call(kernel, inputs, outputs, out_shape, scratch=(), params=PARAMS):
    single = len(outputs) == 1
    return pl.pallas_call(
        kernel,
        in_specs=spec(inputs),
        out_specs=spec(outputs)[0] if single else tuple(spec(outputs)),
        out_shape=out_shape,
        scratch_shapes=list(scratch),
        compiler_params=params,
    )


def shards(
    adjoint_final,
    background,
    friction_velocity,
    wind_direction,
    refraction_rate,
    courant,
    growth_rate,
    dissipation_rate,
    sea_mask,
    interp_index,
    interp_weight,
):
    comp_count = lax.axis_size("comp")
    spectrum = background.reshape(NSTEP, NCOMP, LANES)
    held = [pltpu.VMEM((LOCAL, NX, LANES), jnp.float32), pltpu.SemaphoreType.DMA((LOCAL,))]
    sems = pltpu.SemaphoreType.DMA((CHUNKS,))
    by_row = call(
        by_row_kernel, "h", "h", f32(NCOMP, LANES), [held[0], sems, pltpu.VMEM((NCOMP, LANES), jnp.float32), sems], WHOLE
    )(adjoint_final)
    points = lax.all_to_all(by_row.reshape(NCOMP, 1, LANES), "comp", split_axis=0, concat_axis=0, tiled=True)
    points = points.reshape(NCOMP, LANES)
    coef, spread, vec, face, owner, cell = call(
        prepare_kernel,
        "vvvvsssvvv",
        "vvvvvv",
        (
            f32(13, NFREQ, LANES),
            f32(NSTEP, NDIR, LANES),
            f32(8, LANES),
            f32(2, NX, LANES),
            jax.ShapeDtypeStruct((NX, 4 * LANES), jnp.bfloat16),
            f32(PART, 4 * LANES),
        ),
    )(
        spectrum,
        friction_velocity.reshape(NSTEP, LANES),
        wind_direction.reshape(NSTEP, LANES),
        refraction_rate.reshape(NFREQ, LANES),
        courant,
        growth_rate,
        dissipation_rate,
        sea_mask,
        interp_index.reshape(4, LANES),
        interp_weight.reshape(4, LANES),
    )
    moved, one, two, edge, stress = call(
        first_source_kernel,
        "vvvvv",
        "vvvvv",
        (f32(NCOMP, LANES), f32(HALF, LANES), f32(HALF, LANES), f32(NFREQ, LANES), f32(8, LANES)),
    )(points, spectrum, coef, spread, vec)
    swap = [(0, 1), (1, 0)]
    last = comp_count - 1
    pairs = [(2 * i + t, 2 * (((i + 1) ^ 1) - 1) + t) for i in range(1, last) for t in range(2)]
    pairs += [(2 * i + t, 2 * i + 1 - t) for i in (0, last) for t in range(2)]
    one = lax.ppermute(one, "comp", [(i, i ^ 1) for i in range(comp_count)])
    two = lax.ppermute(two, ("comp", "tile"), pairs)
    edge = lax.ppermute(edge, "tile", swap)
    done, done_sums = call(first_half_kernel, "v" * 6, "vv", (f32(HALF, LANES), f32(16, LANES)))(
        moved, one, edge, spectrum, coef, spread
    )
    sent = call(
        second_source_kernel,
        "v" * 12,
        "v",
        f32(NX * SENT, LANES),
        [pltpu.VMEM((HALF, LANES), jnp.float32), pltpu.VMEM((16, LANES), jnp.float32)],
    )(moved, two, edge, spectrum, coef, spread, vec, stress, owner, cell, done, done_sums)
    arrived = lax.all_to_all(sent.reshape(NX * SENT, 1, LANES), "comp", split_axis=0, concat_axis=0, tiled=True)
    arrived = arrived.reshape(NX * SENT, LANES)
    mine = call(edges_kernel, "v", "v", f32(NX + 8, LANES))(arrived)
    theirs = lax.ppermute(mine, "tile", swap)
    adjoint, gradient = call(
        last_kernel, "vvvv", "hv", (f32(LOCAL, NX, LANES), f32(NSTEP, CELLS // 2)), held
    )(arrived, mine, theirs, face)
    return adjoint, gradient.T


def solution(mesh):
    in_specs = (
        P("comp", None, "tile"),
        P(None, None, "comp", "tile"),
        P(None, "comp", "tile"),
        P(None, "comp", "tile"),
        P(None, "comp", "tile"),
        P(),
        P(),
        P(),
        P(),
        P(None, "comp", "tile"),
        P(None, "comp", "tile"),
    )
    out_specs = (P("comp", None, "tile"), P(("comp", "tile"), None))
    return jax.shard_map(shards, mesh=mesh, in_specs=in_specs, out_specs=out_specs, check_vma=False)
```

```python
import math

import jax
import jax.numpy as jnp
import numpy as np
from jax import lax
from jax.experimental import pallas as pl
from jax.experimental.pallas import tpu as pltpu
from jax.sharding import PartitionSpec as P

NDIR = 36
NFREQ = 32
NSTEP = 2
NCOMP = NDIR * NFREQ
NX = 128
LANES = 128
LOCAL = 9
QUART = 4
SENT = LOCAL + 1
CHUNKS = 2
CELLS = 16

THETA = np.arange(NDIR) * (2.0 * math.pi / NDIR)
COS = [0.0 if d % 18 == 9 else math.cos(t) for d, t in enumerate(THETA)]
SIN = [0.0 if d % 18 == 0 else math.sin(t) for d, t in enumerate(THETA)]
EAST = list(range(27, NDIR)) + list(range(0, 9))
WEST = list(range(9, 27))
assert all(COS[d] >= 0 for d in EAST) and all(COS[d] <= 0 for d in WEST)
assert all(SIN[d] >= 0 for d in range(18)) and all(SIN[d] <= 0 for d in range(18, 36))
ORDER = EAST + WEST
PLACE = {d: p for p, d in enumerate(ORDER)}
HALF = len(EAST) * NFREQ

GROWTH, DISSIP, KEEP, TURN_NEG, TURN_POS, UP, DOWN, RIGHT, LEFT, GAIN0, GAIN1, LOSS0, LOSS1 = range(13)
GAIN, LOSS = (GAIN0, GAIN1), (LOSS0, LOSS1)
PART = NSTEP * CELLS

PARAMS = pltpu.CompilerParams(vmem_limit_bytes=24 * 1024 * 1024)
WHOLE = pltpu.CompilerParams(vmem_limit_bytes=60 * 1024 * 1024)


def lane_iota(rows):
    return lax.broadcasted_iota(jnp.int32, (rows, LANES), 1)


def sub_iota(rows):
    return lax.broadcasted_iota(jnp.int32, (rows, LANES), 0)


def by_row_kernel(in_ref, out_ref, held_ref, in_sems, rows_ref, out_sems):
    count = NX // CHUNKS
    ins, outs = [], []
    for c in range(CHUNKS):
        part = pl.ds(c * count, count)
        ins.append(pltpu.make_async_copy(in_ref.at[:, part, :], held_ref.at[:, part, :], in_sems.at[c]))
        part = pl.ds(c * count * LOCAL, count * LOCAL)
        outs.append(pltpu.make_async_copy(rows_ref.at[part, :], out_ref.at[part, :], out_sems.at[c]))
        ins[c].start()
    for c in range(CHUNKS):
        ins[c].wait()
        for j in range(LOCAL):
            rows_ref[pl.ds(c * count * LOCAL + j, count, stride=LOCAL), :] = held_ref[j, c * count : (c + 1) * count]
        outs[c].start()
    for copy in outs:
        copy.wait()


def prepare_kernel(
    spectrum_ref, friction_ref, wind_ref, refraction_ref, courant_ref, growth_ref, dissip_ref, mask_ref,
    index_ref, weight_ref, coef_ref, spread_ref, vec_ref, face_ref, owner_ref, cell_ref,
):
    row = lax.axis_index("comp")
    tile = lax.axis_index("tile")
    left_half = mask_ref[:, :LANES].astype(jnp.float32)
    right_half = mask_ref[:, LANES:].astype(jnp.float32)
    first = tile == 0
    own = jnp.where(first, left_half, right_half)
    lane = lane_iota(NX)
    sub = sub_iota(NX)
    other = jnp.where(first, right_half, left_half)
    nxt = jnp.where(lane == LANES - 1, jnp.where(first, pltpu.roll(other, LANES - 1, 1), 0.0), pltpu.roll(own, LANES - 1, 1))
    prv = jnp.where(lane == 0, jnp.where(first, 0.0, pltpu.roll(other, 1, 1)), pltpu.roll(own, 1, 1))
    quarter = row % QUART
    speed = courant_ref[row // QUART]
    up = own * jnp.where(sub == NX - 1, 0.0, pltpu.roll(own, NX - 1, 0))
    down = own * jnp.where(sub == 0, 0.0, pltpu.roll(own, 1, 0))
    right, left = own * nxt, own * prv
    face_ref[0] = speed * jnp.where((quarter == 0) | (quarter == 3), up, down)
    face_ref[1] = speed * jnp.where(quarter < 2, right, left)
    pick = sub == row
    mask, *faces = [
        jnp.sum(jnp.where(pick, value, 0.0), axis=0, keepdims=True) for value in (own, up, down, right, left)
    ]

    sub_f = sub_iota(NFREQ)
    growth = jnp.zeros((NFREQ, LANES), jnp.float32)
    dissip = jnp.zeros((NFREQ, LANES), jnp.float32)
    courant = jnp.zeros((NFREQ, LANES), jnp.float32)
    for f in range(NFREQ):
        at = sub_f == f
        growth = jnp.where(at, growth_ref[f], growth)
        dissip = jnp.where(at, dissip_ref[f], dissip)
        courant = jnp.where(at, courant_ref[f], courant)
    turn = refraction_ref[...]
    coef_ref[GROWTH] = growth
    coef_ref[DISSIP] = dissip
    coef_ref[KEEP] = 1.0 - jnp.abs(turn)
    coef_ref[TURN_NEG] = jnp.minimum(turn, 0.0)
    coef_ref[TURN_POS] = jnp.maximum(turn, 0.0)
    for k, name in enumerate((UP, DOWN, RIGHT, LEFT)):
        coef_ref[name] = courant * faces[k]
    vec_ref[...] = jnp.zeros_like(vec_ref)
    vec_ref[2:3] = mask
    theta = sub_iota(NDIR).astype(jnp.float32) * (2.0 * math.pi / NDIR)
    for n in range(NSTEP):
        total = jnp.zeros((8, LANES), jnp.float32)
        for k in range(NCOMP // 8):
            total = total + spectrum_ref[n, pl.ds(8 * k, 8), :]
        energy = jnp.sum(total, axis=0, keepdims=True) / NFREQ
        vec_ref[n : n + 1] = (2.0 / NFREQ) * energy * mask
        coef_ref[GAIN[n]] = growth * (friction_ref[n : n + 1] * mask)
        coef_ref[LOSS[n]] = mask - dissip * (energy * energy * mask)
        spread_ref[n] = jnp.maximum(jnp.cos(theta - wind_ref[n : n + 1]), 0.0)

    sub_c = sub_iota(PART)
    for corner in range(4):
        lanes = slice(corner * LANES, (corner + 1) * LANES)
        index = index_ref[corner : corner + 1, :]
        owner_ref[:, lanes] = jnp.where(sub == index // CELLS, 1.0, 0.0).astype(jnp.bfloat16)
        cell_ref[:, lanes] = jnp.where(sub_c % CELLS == index % CELLS, weight_ref[corner : corner + 1, :], 0.0)


def source_sums(adjoint_of, spectrum_ref, coef_ref, spread_ref, vec_ref, step):
    damped = jnp.zeros((8, LANES), jnp.float32)
    stress = jnp.zeros((8, LANES), jnp.float32)
    for b in range(NFREQ // 8):
        plain = jnp.zeros((8, LANES), jnp.float32)
        spread = jnp.zeros((8, LANES), jnp.float32)
        for p, d in enumerate(ORDER):
            product = spectrum_ref[step, pl.ds(8 * b * NDIR + d, 8, stride=NDIR), :] * adjoint_of(b, p, d)
            plain = plain + product
            spread = spread + spread_ref[step, d : d + 1, :] * product
        damped = damped + coef_ref[DISSIP, 8 * b : 8 * b + 8] * plain
        stress = stress + coef_ref[GROWTH, 8 * b : 8 * b + 8] * spread
    damped = jnp.sum(damped, axis=0, keepdims=True)
    stress = jnp.sum(stress, axis=0, keepdims=True)
    return vec_ref[step : step + 1] * damped, vec_ref[2:3] * stress


def source_update(adjoint_of, store, coef_ref, spread_ref, shared, step):
    shared = jnp.broadcast_to(shared, (8, LANES))
    for b in range(NFREQ // 8):
        rows = slice(8 * b, 8 * b + 8)
        gain, loss = coef_ref[GAIN[step], rows], coef_ref[LOSS[step], rows]
        keep, neg, pos = coef_ref[KEEP, rows], coef_ref[TURN_NEG, rows], coef_ref[TURN_POS, rows]

        def updated(d):
            return adjoint_of(b, PLACE[d], d) * (loss + gain * spread_ref[step, d : d + 1, :]) - shared

        before, here, first = updated(ORDER[-1]), updated(ORDER[0]), None
        first = here
        for p, d in enumerate(ORDER):
            after = updated(ORDER[p + 1]) if p + 1 < NDIR else first
            store(b, p, d, keep * here - neg * before + pos * after)
            before, here = here, after


def first_source_kernel(
    adjoint_ref, spectrum_ref, coef_ref, spread_ref, vec_ref, moved_ref, one_ref, two_ref, edge_ref, stress_ref
):
    step = NSTEP - 1

    def adjoint_of(b, p, d):
        return adjoint_ref[pl.ds(8 * b * NDIR + d, 8, stride=NDIR), :]

    shared, stress = source_sums(adjoint_of, spectrum_ref, coef_ref, spread_ref, vec_ref, step)
    stress_ref[...] = jnp.broadcast_to(stress, (8, LANES))
    lane = lane_iota(8)
    half = NDIR // 2
    odd = lax.axis_index("comp") % 2
    for parity in range(2):

        @pl.when(odd == parity)
        def _():
            edges = [jnp.zeros((8, LANES), jnp.float32) for _ in range(NFREQ // 8)]

            def store(b, p, d, value):
                moved_ref[pl.ds(p * NFREQ + 8 * b, 8), :] = value
                sent_ref = one_ref if (p < half) == (parity == 1) else two_ref
                sent_ref[pl.ds(p % half * NFREQ + 8 * b, 8), :] = value
                column = value[:, :1] if SIN[d] >= 0 else value[:, LANES - 1 :]
                edges[b] = jnp.where(lane == p, column, edges[b])

            source_update(adjoint_of, store, coef_ref, spread_ref, shared, step)
            for b in range(NFREQ // 8):
                edge_ref[8 * b : 8 * b + 8] = edges[b]


def propagate_half(east, moved_ref, near_ref, edge_ref, spectrum_ref, coef_ref, spread_ref, half_ref, sums_ref):
    step = 0
    lane = lane_iota(8)
    half = NDIR // 2
    face, start = (UP, 0) if east else (DOWN, half)
    damped = jnp.zeros((8, LANES), jnp.float32)
    stress = jnp.zeros((8, LANES), jnp.float32)
    for b in range(NFREQ // 8):
        rows = slice(8 * b, 8 * b + 8)
        plain = jnp.zeros((8, LANES), jnp.float32)
        spread = jnp.zeros((8, LANES), jnp.float32)
        for at in range(half):
            p = start + at
            d = ORDER[p]
            centre = moved_ref[pl.ds(p * NFREQ + 8 * b, 8), :]
            row = near_ref[pl.ds(at * NFREQ + 8 * b, 8), :]
            arrived = edge_ref[rows, p : p + 1]
            if SIN[d] >= 0:
                side, column = RIGHT, jnp.where(lane == LANES - 1, arrived, pltpu.roll(centre, LANES - 1, 1))
            else:
                side, column = LEFT, jnp.where(lane == 0, arrived, pltpu.roll(centre, 1, 1))
            value = (
                centre
                + abs(COS[d]) * (coef_ref[face, rows] * (row - centre))
                + abs(SIN[d]) * (coef_ref[side, rows] * (column - centre))
            )
            half_ref[pl.ds(at * NFREQ + 8 * b, 8), :] = value
            product = spectrum_ref[step, pl.ds(8 * b * NDIR + d, 8, stride=NDIR), :] * value
            plain = plain + product
            spread = spread + spread_ref[step, d : d + 1, :] * product
        damped = damped + coef_ref[DISSIP, rows] * plain
        stress = stress + coef_ref[GROWTH, rows] * spread
    sums_ref[:8] = damped
    sums_ref[8:] = stress


def first_half_kernel(moved_ref, one_ref, edge_ref, spectrum_ref, coef_ref, spread_ref, half_ref, sums_ref):
    odd = lax.axis_index("comp") % 2
    for parity, east in ((0, True), (1, False)):

        @pl.when(odd == parity)
        def _():
            propagate_half(east, moved_ref, one_ref, edge_ref, spectrum_ref, coef_ref, spread_ref, half_ref, sums_ref)


def second_source_kernel(
    moved_ref, two_ref, edge_ref, spectrum_ref, coef_ref, spread_ref, vec_ref, stress_ref,
    owner_ref, cell_ref, done_ref, done_sums_ref, out_ref, half_ref, sums_ref,
):
    step = 0
    odd = lax.axis_index("comp") % 2
    even = jnp.broadcast_to(odd, (8, LANES)) == 0
    for parity, east in ((0, False), (1, True)):

        @pl.when(odd == parity)
        def _():
            propagate_half(east, moved_ref, two_ref, edge_ref, spectrum_ref, coef_ref, spread_ref, half_ref, sums_ref)

    damped = jnp.sum(done_sums_ref[:8] + sums_ref[:8], axis=0, keepdims=True)
    stress = jnp.sum(done_sums_ref[8:] + sums_ref[8:], axis=0, keepdims=True)
    shared, stress = vec_ref[step : step + 1] * damped, vec_ref[2:3] * stress

    values = jnp.concatenate(
        [
            cell_ref[CELLS * n : CELLS * n + CELLS, :] * jnp.concatenate([row] * 4, axis=1)
            for n, row in enumerate((stress, stress_ref[:1]))
        ],
        axis=0,
    )
    parts = []
    for _ in range(3):
        parts.append(values.astype(jnp.bfloat16))
        values = values - parts[-1].astype(jnp.float32)
    parts.append(jnp.zeros_like(parts[0]))
    cells = lax.dot_general(
        owner_ref[...], jnp.concatenate(parts, axis=0), (((1,), (1,)), ((), ())), preferred_element_type=jnp.float32
    )
    out_ref[pl.ds(LOCAL, NX, stride=SENT), :] = cells

    def adjoint_of(b, p, d):
        east = p < NDIR // 2
        rows = pl.ds((p if east else p - NDIR // 2) * NFREQ + 8 * b, 8)
        done, here = done_ref[rows, :], half_ref[rows, :]
        return jnp.where(even, done, here) if east else jnp.where(even, here, done)

    def store(b, p, d, value):
        at = 8 * b * QUART * SENT + d // LOCAL * SENT + d % LOCAL
        out_ref[pl.ds(at, 8, stride=QUART * SENT), :] = value

    source_update(adjoint_of, store, coef_ref, spread_ref, shared, step)


def edges_kernel(arrived_ref, out_ref):
    lane = lane_iota(NX)
    quarter = lax.axis_index("comp") % QUART
    for north in (True, False):

        @pl.when((quarter < 2) == north)
        def _():
            edges = jnp.zeros((NX, LANES), jnp.float32)
            for j in range(LOCAL):
                value = arrived_ref[pl.ds(j, NX, stride=SENT), :]
                edges = jnp.where(lane == j, value[:, :1] if north else value[:, LANES - 1 :], edges)
            out_ref[:NX] = edges

    cells = arrived_ref[pl.ds(LOCAL, NX, stride=SENT), :]
    out_ref[NX:] = jnp.broadcast_to(jnp.sum(cells, axis=0, keepdims=True), (8, LANES))


def last_kernel(arrived_ref, mine_ref, edges_ref, face_ref, adjoint_ref, gradient_ref, held_ref, sems):
    tile = lax.axis_index("tile")
    quarter = lax.axis_index("comp") % QUART
    lane = lane_iota(NX)
    copies = [pltpu.make_async_copy(held_ref.at[j], adjoint_ref.at[j], sems.at[j]) for j in range(LOCAL)]
    for q in range(QUART):

        @pl.when(quarter == q)
        def _():
            for j in range(LOCAL):
                d = q * LOCAL + j
                centre = arrived_ref[pl.ds(j, NX, stride=SENT), :]
                arrived = edges_ref[:NX, j : j + 1]
                row = pltpu.roll(centre, NX - 1 if d in EAST else 1, 0)
                if SIN[q * LOCAL + 1] > 0:
                    column = jnp.where(lane == LANES - 1, arrived, pltpu.roll(centre, LANES - 1, 1))
                else:
                    column = jnp.where(lane == 0, arrived, pltpu.roll(centre, 1, 1))
                held_ref[j] = (
                    centre
                    + abs(COS[d]) * (face_ref[0] * (row - centre))
                    + abs(SIN[d]) * (face_ref[1] * (column - centre))
                )
                copies[j].start()

    cells = mine_ref[NX:] + edges_ref[NX:]
    cells = cells + pltpu.roll(cells, LANES - PART, 1) + pltpu.roll(cells, LANES - 2 * PART, 1)
    for n in range(NSTEP):
        at = pltpu.roll(cells, LANES - n * CELLS - tile * (CELLS // 2), 1)
        gradient_ref[n : n + 1, :] = at[:1, : CELLS // 2]
    for copy in copies:
        copy.wait()


def f32(*shape):
    return jax.ShapeDtypeStruct(shape, jnp.float32)


SPACES = {"s": pltpu.SMEM, "v": pltpu.VMEM, "h": pltpu.HBM}


def spec(spaces):
    return [pl.BlockSpec(memory_space=SPACES[space]) for space in spaces]


def call(kernel, inputs, outputs, out_shape, scratch=(), params=PARAMS):
    single = len(outputs) == 1
    return pl.pallas_call(
        kernel,
        in_specs=spec(inputs),
        out_specs=spec(outputs)[0] if single else tuple(spec(outputs)),
        out_shape=out_shape,
        scratch_shapes=list(scratch),
        compiler_params=params,
    )


def shards(
    adjoint_final,
    background,
    friction_velocity,
    wind_direction,
    refraction_rate,
    courant,
    growth_rate,
    dissipation_rate,
    sea_mask,
    interp_index,
    interp_weight,
):
    comp_count = lax.axis_size("comp")
    spectrum = background.reshape(NSTEP, NCOMP, LANES)
    held = [pltpu.VMEM((LOCAL, NX, LANES), jnp.float32), pltpu.SemaphoreType.DMA((LOCAL,))]
    sems = pltpu.SemaphoreType.DMA((CHUNKS,))
    by_row = call(
        by_row_kernel, "h", "h", f32(NCOMP, LANES), [held[0], sems, pltpu.VMEM((NCOMP, LANES), jnp.float32), sems], WHOLE
    )(adjoint_final)
    points = lax.all_to_all(by_row.reshape(NCOMP, 1, LANES), "comp", split_axis=0, concat_axis=0, tiled=True)
    points = points.reshape(NCOMP, LANES)
    coef, spread, vec, face, owner, cell = call(
        prepare_kernel,
        "vvvvsssvvv",
        "vvvvvv",
        (
            f32(13, NFREQ, LANES),
            f32(NSTEP, NDIR, LANES),
            f32(8, LANES),
            f32(2, NX, LANES),
            jax.ShapeDtypeStruct((NX, 4 * LANES), jnp.bfloat16),
            f32(PART, 4 * LANES),
        ),
    )(
        spectrum,
        friction_velocity.reshape(NSTEP, LANES),
        wind_direction.reshape(NSTEP, LANES),
        refraction_rate.reshape(NFREQ, LANES),
        courant,
        growth_rate,
        dissipation_rate,
        sea_mask,
        interp_index.reshape(4, LANES),
        interp_weight.reshape(4, LANES),
    )
    moved, one, two, edge, stress = call(
        first_source_kernel,
        "vvvvv",
        "vvvvv",
        (f32(NCOMP, LANES), f32(HALF, LANES), f32(HALF, LANES), f32(NFREQ, LANES), f32(8, LANES)),
    )(points, spectrum, coef, spread, vec)
    swap = [(0, 1), (1, 0)]
    last = comp_count - 1
    pairs = [(2 * i + t, 2 * (((i + 1) ^ 1) - 1) + t) for i in range(1, last) for t in range(2)]
    pairs += [(2 * i + t, 2 * i + 1 - t) for i in (0, last) for t in range(2)]
    one = lax.ppermute(one, "comp", [(i, i ^ 1) for i in range(comp_count)])
    two = lax.ppermute(two, ("comp", "tile"), pairs)
    edge = lax.ppermute(edge, "tile", swap)
    done, done_sums = call(first_half_kernel, "v" * 6, "vv", (f32(HALF, LANES), f32(16, LANES)))(
        moved, one, edge, spectrum, coef, spread
    )
    sent = call(
        second_source_kernel,
        "v" * 12,
        "v",
        f32(NX * SENT, LANES),
        [pltpu.VMEM((HALF, LANES), jnp.float32), pltpu.VMEM((16, LANES), jnp.float32)],
    )(moved, two, edge, spectrum, coef, spread, vec, stress, owner, cell, done, done_sums)
    arrived = lax.all_to_all(sent.reshape(NX * SENT, 1, LANES), "comp", split_axis=0, concat_axis=0, tiled=True)
    arrived = arrived.reshape(NX * SENT, LANES)
    mine = call(edges_kernel, "v", "v", f32(NX + 8, LANES))(arrived)
    theirs = lax.ppermute(mine, "tile", swap)
    adjoint, gradient = call(
        last_kernel, "vvvv", "hv", (f32(LOCAL, NX, LANES), f32(NSTEP, CELLS // 2)), held
    )(arrived, mine, theirs, face)
    return adjoint, gradient.T


def solution(mesh):
    in_specs = (
        P("comp", None, "tile"),
        P(None, None, "comp", "tile"),
        P(None, "comp", "tile"),
        P(None, "comp", "tile"),
        P(None, "comp", "tile"),
        P(),
        P(),
        P(),
        P(),
        P(None, "comp", "tile"),
        P(None, "comp", "tile"),
    )
    out_specs = (P("comp", None, "tile"), P(("comp", "tile"), None))
    return jax.shard_map(shards, mesh=mesh, in_specs=in_specs, out_specs=out_specs, check_vma=False)
```
